256 devices in a mesh: sector: 8 (over x, core), slab: 32 (over y, z).
Axes of the slice: x: 4, y: 4, z: 8, core: 2. Of those that a mesh axis runs over, the one named last changes fastest.
Arguments:
- pressure: float32 [128, 512, 128], P('slab', 'sector'), may hold values from -6 to 6
- saturation: float32 [2, 128, 512, 128], P(None, 'slab', 'sector'), may hold values from 0.05 to 0.45
- old_mass: float32 [3, 128, 512, 128], P(None, 'slab', 'sector'), may hold values from 0 to 2.4
- pore_volume: float32 [128, 512, 128], P('slab', 'sector'), may hold values from 0.5 to 2
- transmissibility: float32 [3, 128, 512, 128], P(None, 'slab', 'sector'), may hold values from 0.2 to 5
- upwind_bits: int32 [128, 512, 128], P('slab', 'sector'), may hold values from 0 to 511
- fault_cell: int32 [32, 8, 8, 1024], P('slab', 'sector'), may hold values from 0 to 32767
- fault_count: int32 [32, 8, 8], P('slab', 'sector'), may hold values from 0 to 1024, as said below
- fault_trans: float32 [32, 8, 8, 1024], P('slab', 'sector'), as said below
- fault_upwind: int32 [32, 8, 8, 1024], P('slab', 'sector'), may hold values from 0 to 7, as said below
Outputs:
- residual: float32 [3, 128, 512, 128], P(None, 'slab', 'sector')
- pressure_update: float32 [128, 512, 128], P('slab', 'sector')
The draws below stay inside these ranges and needn't reach their ends.
Inputs may be any that keep to these rules, and one draw needn't show every extreme that they name: `fault_count`: symmetric in its two sector dimensions, zero where they are equal; for every slab index some pair of sectors has exactly 1024 live slots. `fault_trans`: entry [t, s, e, j] equals entry [t, e, s, j]. `fault_upwind`: for s different from e, entries [t, s, e, j] and [t, e, s, j] add up to 7.
All inputs are finite; a program needn't handle non-finite values.
Results may differ from the reference program's by a relative error of at most 0.0003.
Values sent between devices are 32-bit elements; how exact they have to be, the bound alone decides.
A program may use at most 128 MiB of HBM per device.

```python
import math
import jax
import jax.numpy as jnp
from jax import lax

CZ = 4
CX = 64
CY = 128
CAP = 1024
SWEEPS = 4
NZ = 128
NX = 512
N_SECTOR = 8
N_SLAB = 32


def draw_fault_count(key, part):
    shape = (N_SLAB, N_SECTOR, N_SECTOR)
    raw = jax.random.randint(jax.random.fold_in(key, 11), shape, CAP // 4, CAP + 1)
    sender = lax.broadcasted_iota(jnp.int32, shape, 1)
    target = lax.broadcasted_iota(jnp.int32, shape, 2)
    mirrored = jnp.where(sender < target, raw, jnp.swapaxes(raw, 1, 2))
    first = jax.random.randint(jax.random.fold_in(key, 12), (N_SLAB, 1, 1), 0, N_SECTOR)
    offset = jax.random.randint(jax.random.fold_in(key, 13), (N_SLAB, 1, 1), 1, N_SECTOR)
    second = (first + offset) % N_SECTOR
    full_pair = (sender == first) & (target == second) | (sender == second) & (target == first)
    counts = jnp.where(full_pair, CAP, mirrored)
    return jnp.where(sender == target, 0, counts).astype(jnp.int32)


def draw_fault_trans(key, part):
    shape = (N_SLAB, N_SECTOR, N_SECTOR, CAP)
    raw = jnp.exp(jax.random.uniform(key, shape, jnp.float32, math.log(0.2), math.log(5.0)))
    sender = lax.broadcasted_iota(jnp.int32, shape, 1)
    target = lax.broadcasted_iota(jnp.int32, shape, 2)
    return jnp.where(sender < target, raw, jnp.swapaxes(raw, 1, 2)).astype(jnp.float32)


def draw_fault_upwind(key, part):
    shape = (N_SLAB, N_SECTOR, N_SECTOR, CAP)
    raw = jax.random.randint(key, shape, 0, 8)
    sender = lax.broadcasted_iota(jnp.int32, shape, 1)
    target = lax.broadcasted_iota(jnp.int32, shape, 2)
    return jnp.where(sender < target, raw, 7 - jnp.swapaxes(raw, 1, 2)).astype(jnp.int32)


def reservoir_state(key):
    shape = (NZ, NX, CY)
    pore_key = jax.random.fold_in(key, 21)
    fluid_key = jax.random.fold_in(key, 22)
    change_key = jax.random.fold_in(key, 23)
    pore = jnp.exp(jax.random.uniform(pore_key, shape, jnp.float32, math.log(0.5), math.log(2.0)))
    fluid = jnp.clip(0.25 + 0.08 * jax.random.normal(fluid_key, (2,) + shape, jnp.float32), 0.05, 0.45)
    change = jnp.clip(0.12 * jax.random.normal(change_key, (3,) + shape, jnp.float32), -0.3, 0.3)
    phases = jnp.stack([fluid[0], 1.0 - fluid[0] - fluid[1], fluid[1]])
    mass = pore[None] * phases * (1.0 + change)
    return (pore, fluid, mass)


def draw_pore_volume(key, part):
    state = reservoir_state(key)
    return state[0].astype(jnp.float32)


def draw_saturation(key, part):
    state = reservoir_state(key)
    return state[1].astype(jnp.float32)


def draw_old_mass(key, part):
    state = reservoir_state(key)
    return state[2].astype(jnp.float32)


def plant(entries, stream_key, low, top_value):
    longest = entries.shape.index(max(entries.shape))
    spots = []
    for shift in (0, 1):
        where = [jax.random.randint(jax.random.fold_in(stream_key, axis), (), 0, length) for axis, length in enumerate(entries.shape)]
        where[longest] = (where[longest] + shift) % entries.shape[longest]
        spots.append(tuple(where))
    return entries.at[spots[0]].set(low).at[spots[1]].set(top_value)


def block_levels(stream_key, extent, pieces, smallest, largest):
    loudness, own = 1.0, jax.random.fold_in(stream_key, 6)
    for axis_at, parts in pieces:
        heights = jnp.exp(jax.random.uniform(jax.random.fold_in(own, axis_at), (parts,), jnp.float32, smallest / len(pieces), largest / len(pieces)))
        loudness = loudness * jnp.repeat(heights, extent[axis_at] // parts).reshape([-1 if axis == axis_at else 1 for axis in range(len(extent))])
    return loudness


def bell_draw(stream_key, dims, width, reach, cuts=(), dtype=jnp.bfloat16):
    array = width * jax.random.normal(stream_key, dims, jnp.float32)
    if cuts:
        array = array * block_levels(stream_key, dims, cuts, -0.22, 0.18)
    return jnp.clip(array, -reach, reach).astype(dtype)


def setup_inputs(seed: int = 0) -> dict:
    keys = jax.random.split(jax.random.key(seed), 11)
    pressure = bell_draw(keys[0], (NZ, NX, CY), 1.0, 6.0, ((0, 32), (1, 8)), jnp.float32)
    saturation = draw_saturation(jax.random.fold_in(keys[10], 71), 0)
    old_mass = draw_old_mass(jax.random.fold_in(keys[10], 71), 0)
    pore_volume = draw_pore_volume(jax.random.fold_in(keys[10], 71), 0)
    transmissibility = jnp.clip(jnp.exp(math.log(5.0) - 3.218876 * jax.random.uniform(keys[4], (3, NZ, NX, CY), jnp.float32) ** block_levels(keys[4], (3, NZ, NX, CY), ((1, 32), (2, 8)), -0.2, 0.2)), 0.2, 5.0)
    upwind_bits = plant(jax.random.randint(keys[5], (NZ, NX, CY), 0, 512), jax.random.fold_in(keys[5], 1), 0, 511).astype(jnp.int32)
    fault_cell = plant(jax.random.randint(keys[6], (N_SLAB, N_SECTOR, N_SECTOR, CAP), 0, CZ * CX * CY), jax.random.fold_in(keys[6], 1), 0, (CZ * CX * CY) - 1).astype(jnp.int32)
    fault_count = draw_fault_count(jax.random.fold_in(keys[10], 71), 0)
    fault_trans = draw_fault_trans(jax.random.fold_in(keys[10], 71), 0)
    fault_upwind = draw_fault_upwind(jax.random.fold_in(keys[10], 71), 0)
    return dict(pressure=pressure, saturation=saturation, old_mass=old_mass, pore_volume=pore_volume, transmissibility=transmissibility, upwind_bits=upwind_bits, fault_cell=fault_cell, fault_count=fault_count, fault_trans=fault_trans, fault_upwind=fault_upwind)


COMPRESS = (0.0002, 0.0005, 0.002)
VISCOSITY = (1.0, 3.0, 0.5)
RELAXATION = 2.0 / 3.0

def phase_state(pressure, saturation):
    water = saturation[0]
    gas_part = saturation[1]
    saturations = jnp.stack([water, 1.0 - water - gas_part, gas_part])
    mobility = jnp.stack([saturations[phase] * saturations[phase] / VISCOSITY[phase] for phase in range(3)])
    return (saturations, mobility)

def accumulation(pressure, saturations, pore_volume, old_mass):
    masses = jnp.stack([pore_volume * saturations[phase] * (1.0 + COMPRESS[phase] * pressure) for phase in range(3)])
    storage = pore_volume * (saturations[0] * COMPRESS[0] + saturations[1] * COMPRESS[1] + saturations[2] * COMPRESS[2])
    return (masses - old_mass, storage)

def upwind_flags(words, first_bit):
    return jnp.stack([jnp.bitwise_and(jnp.right_shift(words, first_bit + phase), 1) for phase in range(3)])

def face_terms(low_pressure, low_mobility, low_trans, low_words, high_pressure, high_mobility, face_valid, direction):
    flags = upwind_flags(low_words, 3 * direction)
    upstream = jnp.where(flags == 1, low_mobility, high_mobility)
    weight = low_trans * face_valid
    face_flux = weight * upstream * (low_pressure - high_pressure)
    coupling = weight * (upstream[0] + upstream[1] + upstream[2])
    return (face_flux, coupling)

def fault_terms(own_pressure, own_mobility, far_pressure, far_mobility, weight, words):
    flags = upwind_flags(words, 0)
    upstream = jnp.where(flags == 1, own_mobility, far_mobility)
    face_flux = weight * upstream * (own_pressure - far_pressure)
    coupling = weight * (upstream[0] + upstream[1] + upstream[2])
    return (face_flux, coupling)

def coarse_solve(coarse_rows):
    store = coarse_rows[0]
    link = coarse_rows[1]
    source = coarse_rows[2]
    zero = jnp.zeros((1,), jnp.float32)
    below = jnp.concatenate([zero, link[:-1]])
    diagonal = store + link + below
    upper = jnp.concatenate([-link[:-1], zero])
    return lax.linalg.tridiagonal_solve(-below, diagonal, upper, source[:, None])[:, 0]

def next_cell(values, axis):
    size = values.shape[axis]
    tail = lax.slice_in_dim(values, 1, size, axis=axis)
    return jnp.concatenate([tail, jnp.zeros_like(lax.slice_in_dim(values, 0, 1, axis=axis))], axis)

def prev_cell(values, axis):
    size = values.shape[axis]
    head = lax.slice_in_dim(values, 0, size - 1, axis=axis)
    return jnp.concatenate([jnp.zeros_like(lax.slice_in_dim(values, 0, 1, axis=axis)), head], axis)

def reference(pressure, saturation, old_mass, pore_volume, transmissibility, upwind_bits, fault_cell, fault_count, fault_trans, fault_upwind):
    grid = pressure.shape
    total_layers, total_rows, column_count = grid
    layer_count = total_layers // N_SLAB
    row_count = total_rows // N_SECTOR
    saturations, mobility = phase_state(pressure, saturation)
    residual, storage = accumulation(pressure, saturations, pore_volume, old_mass)
    diagonal = storage
    couplings = []
    for direction in range(3):
        size = grid[direction]
        face_valid = (lax.broadcasted_iota(jnp.int32, grid, direction) < size - 1).astype(jnp.float32)
        face_flux, coupling = face_terms(pressure, mobility, transmissibility[direction], upwind_bits, next_cell(pressure, direction), next_cell(mobility, direction + 1), face_valid, direction)
        residual = residual + (face_flux - prev_cell(face_flux, direction + 1))
        diagonal = diagonal + (coupling + prev_cell(coupling, direction))
        couplings.append(coupling)
    shape = fault_cell.shape
    slab_id = lax.broadcasted_iota(jnp.int32, shape, 0)
    sector_id = lax.broadcasted_iota(jnp.int32, shape, 1)
    slot_id = lax.broadcasted_iota(jnp.int32, shape, 3)
    layer = fault_cell // (row_count * column_count)
    row_in = fault_cell // column_count % row_count
    column = fault_cell % column_count
    own_index = ((slab_id * layer_count + layer) * total_rows + sector_id * row_count + row_in) * column_count + column
    far_index = jnp.swapaxes(own_index, 1, 2)
    slot_live = (slot_id < fault_count[..., None]).astype(jnp.float32)
    own_flat = own_index.reshape(-1)
    far_flat = far_index.reshape(-1)
    flat_pressure = pressure.reshape(-1)
    flat_mobility = mobility.reshape(3, -1)
    fault_flux, fault_link = fault_terms(flat_pressure[own_flat], flat_mobility[:, own_flat], flat_pressure[far_flat], flat_mobility[:, far_flat], (fault_trans * slot_live).reshape(-1), fault_upwind.reshape(-1))
    residual = residual.reshape(3, -1).at[:, own_flat].add(fault_flux).reshape(residual.shape)
    diagonal = diagonal.reshape(-1).at[own_flat].add(fault_link).reshape(grid)
    pressure_rhs = -(residual[0] + residual[1] + residual[2])
    coarse_rows = jnp.stack([storage.sum(axis=(1, 2)), couplings[0].sum(axis=(1, 2)), pressure_rhs.sum(axis=(1, 2))])
    coarse = coarse_solve(coarse_rows)
    update = jnp.broadcast_to(coarse[:, None, None], grid)

    def apply_operator(field):
        image = diagonal * field
        for direction in range(3):
            image = image - (couplings[direction] * next_cell(field, direction) + prev_cell(couplings[direction], direction) * prev_cell(field, direction))
        far_values = field.reshape(-1)[far_flat]
        extra = jnp.zeros((field.size,), jnp.float32).at[own_flat].add(fault_link * far_values).reshape(grid)
        return image - extra
    for sweep in range(SWEEPS):
        update = update + RELAXATION * (pressure_rhs - apply_operator(update)) / diagonal
    return (residual, update)
```

```python
import functools

import jax
import jax.numpy as jnp
from jax import lax
from jax.experimental import pallas as pl
from jax.experimental.pallas import tpu as pltpu
from jax.sharding import PartitionSpec as P

COMPRESS = (0.0002, 0.0005, 0.002)
VISCOSITY = (1.0, 3.0, 0.5)
RELAXATION = 2.0 / 3.0
SWEEPS = 4

BF = jnp.bfloat16
F32 = jnp.float32
MESH = pl.DeviceIdType.MESH

LAYERS, ROWS, COLS = 4, 64, 128
CELLS_HI = LAYERS * ROWS
SLOTS = 1024
CHUNKS = SLOTS // 128


def split(value, count):
    parts = []
    for _ in range(count - 1):
        part = value.astype(BF)
        parts.append(part)
        value = value - part.astype(F32)
    parts.append(value.astype(BF))
    return parts


def mobilities(s_water, s_gas):
    s_oil = 1.0 - s_water - s_gas
    return [s * s * (1.0 / v) for s, v in zip((s_water, s_oil, s_gas), VISCOSITY)]


def face(p_low, m_low, weight, words, p_high, m_high, first_bit):
    drop = p_low - p_high
    fluxes, total = [], None
    for a in range(3):
        flag = jnp.bitwise_and(words, 1 << (first_bit + a)) != 0
        part = weight * jnp.where(flag, m_low[a], m_high[a])
        fluxes.append(part * drop)
        total = part if total is None else total + part
    return fluxes, total


def kernel(
    n_sector, n_slab,
    p_ref, s_ref, om_ref, pv_ref, tr_ref, bits_ref, fc_ref, cnt_ref, ft_ref, fu_ref,
    res_ref, out_ref, *,
    oh, ohlo, fsplit, acc, cell, fweight, fup, own, far, link, vals,
    up_stage, dn_stage, halo_lo, halo_hi, rup_stage, rdn_stage, rhalo_lo, rhalo_hi,
    asend, arecv, bsend, brecv,
    cz, cxu, cxd, cyu, cyd, storage, rhs, inv, ubuf, part,
    uown, urecv, usend, zlo, zhi, xup, xdn, xlo, xhi,
    f_ss, f_rs, h_ss, h_rs, a_ss, a_rs, b_ss, b_rs, u_ss, u_rs, w_ss, w_rs,
):
    me = lax.axis_index("sector")
    t = lax.axis_index("slab")
    others = n_sector - 1
    s_next = lax.rem(me + 1, n_sector)
    s_prev = lax.rem(me + n_sector - 1, n_sector)
    t_next = lax.rem(t + 1, n_slab)
    t_prev = lax.rem(t + n_slab - 1, n_slab)

    def copy(src, dst, ss, rs, device):
        return pltpu.make_async_remote_copy(
            src_ref=src, dst_ref=dst, send_sem=ss, recv_sem=rs,
            device_id=device, device_id_type=MESH,
        )

    def sector_of(d):
        return lax.rem(me + d, n_sector)

    barrier = pltpu.get_barrier_semaphore()

    @pl.loop(1, n_sector)
    def _(d):
        pl.semaphore_signal(barrier, inc=1, device_id=(sector_of(d), t), device_id_type=MESH)

    @pl.loop(1, n_slab)
    def _(k):
        pl.semaphore_signal(
            barrier, inc=1, device_id=(me, lax.rem(t + k, n_slab)), device_id_type=MESH
        )

    top = LAYERS - 1
    for i, plane in enumerate((p_ref[top], s_ref[0, top], s_ref[1, top], tr_ref[0, top])):
        up_stage[i] = plane
    up_stage[4] = bits_ref[top].astype(F32)
    for i, plane in enumerate((p_ref[0], s_ref[0, 0], s_ref[1, 0])):
        dn_stage[i] = plane
    last = ROWS - 1
    for k in range(LAYERS):
        for i, row in enumerate(
            (p_ref[k, last:], s_ref[0, k, last:], s_ref[1, k, last:], tr_ref[1, k, last:])
        ):
            rup_stage[i, k : k + 1, :] = row
        rup_stage[4, k : k + 1, :] = bits_ref[k, last:].astype(F32)
        for i, row in enumerate((p_ref[k, :1], s_ref[0, k, :1], s_ref[1, k, :1])):
            rdn_stage[i, k : k + 1, :] = row

    lane = lax.broadcasted_iota(jnp.int32, (1, 128), 1)
    counts = [cnt_ref[0, 0, sector_of(d)] for d in range(1, n_sector)]
    turn = lax.rem(n_sector - me, n_sector)
    for b in range(CHUNKS):
        span = slice(b * 128, (b + 1) * 128)
        cells = pltpu.roll(fc_ref[0, 0, :, span], turn, 0)
        flags = pltpu.roll(fu_ref[0, 0, :, span], turn, 0)
        trans = pltpu.roll(ft_ref[0, 0, :, span], turn, 0)
        for d in range(others):
            row = slice(d + 1, d + 2)
            cell[d, b : b + 1, :] = cells[row]
            fup[d, b : b + 1, :] = flags[row]
            fweight[d, b : b + 1, :] = jnp.where(lane + b * 128 < counts[d], trans[row], 0.0)

    for i, field in enumerate((p_ref, s_ref.at[0], s_ref.at[1])):
        flipped = field[...].reshape(CELLS_HI, COLS).T
        for j, piece in enumerate(split(flipped, 3)):
            fsplit[i, j * 128 : (j + 1) * 128, :] = piece

    sub = lax.broadcasted_iota(jnp.int32, (128, 128), 0)
    sub_hi = lax.broadcasted_iota(jnp.int32, (CELLS_HI, 128), 0)

    @pl.loop(0, others)
    def _(d):
        for b in range(CHUNKS):
            span = slice(b * 128, (b + 1) * 128)
            c = cell[d, b : b + 1, :]
            oh[d, :, span] = jnp.where(sub_hi == jnp.right_shift(c, 7), 1.0, 0.0).astype(BF)
            ohlo[d, :, span] = jnp.where(sub == jnp.bitwise_and(c, 127), 1.0, 0.0).astype(BF)

    pl.semaphore_wait(barrier, n_sector - 1 + n_slab - 1)

    halo_copies = [
        copy(up_stage, halo_lo, h_ss.at[0], h_rs.at[0], (me, t_next)),
        copy(dn_stage, halo_hi, h_ss.at[1], h_rs.at[1], (me, t_prev)),
        copy(rup_stage, rhalo_lo, h_ss.at[2], h_rs.at[2], (s_next, t)),
        copy(rdn_stage, rhalo_hi, h_ss.at[3], h_rs.at[3], (s_prev, t)),
    ]
    for c in halo_copies:
        c.start()

    def gather(d, weights, count, store):
        for b in range(CHUNKS // 2):
            picks = oh[d, :, b * 256 : (b + 1) * 256]
            rows = [jnp.bitwise_and(cell[d, 2 * b + k : 2 * b + k + 1, :], 127) for k in range(2)]
            for i, w in enumerate(weights):
                g = jnp.dot(w, picks, preferred_element_type=F32)
                total = g[(count - 1) * 128 :]
                for j in reversed(range(count - 1)):
                    total = g[j * 128 : (j + 1) * 128] + total
                for k in range(2):
                    found = jnp.where(sub == rows[k], total[:, k * 128 : (k + 1) * 128], 0.0)
                    store(i, 2 * b + k, jnp.sum(found, axis=0, keepdims=True))

    def fault_copy(d):
        return copy(own.at[d], far.at[others - 1 - d], f_ss.at[d], f_rs.at[others - 1 - d],
                    (sector_of(d + 1), t))

    @pl.loop(0, others)
    def _(d):
        def store(i, b, row):
            own[d, i, pl.ds(b, 1), :] = row

        gather(d, [fsplit[i] for i in range(3)], 3, store)
        own[d, 3] = jnp.right_shift(cell[d], 13).astype(F32)
        fault_copy(d).start()

    lane2 = lax.broadcasted_iota(jnp.int32, (ROWS, COLS), 1)
    row2 = lax.broadcasted_iota(jnp.int32, (ROWS, COLS), 0)
    not_first_slab = jnp.where(t > 0, 1.0, 0.0).astype(F32)
    not_last_slab = jnp.where(t < n_slab - 1, 1.0, 0.0).astype(F32)
    not_first_sector = jnp.where(me > 0, 1.0, 0.0).astype(F32)
    not_last_sector = jnp.where(me < n_sector - 1, 1.0, 0.0).astype(F32)

    for k in range(LAYERS):
        p = p_ref[k]
        pv = pv_ref[k]
        sw, sg = s_ref[0, k], s_ref[1, k]
        so = 1.0 - sw - sg
        m = mobilities(sw, sg)
        words = bits_ref[k]
        sat = (sw, so, sg)
        st = pv * (sw * COMPRESS[0] + so * COMPRESS[1] + sg * COMPRESS[2])
        storage[k] = st
        res = [pv * sat[a] * (1.0 + COMPRESS[a] * p) - om_ref[a, k] for a in range(3)]
        flux, coupling = face(
            p, m, jnp.where(lane2 < COLS - 1, tr_ref[2, k], 0.0), words,
            pltpu.roll(p, COLS - 1, 1), [pltpu.roll(x, COLS - 1, 1) for x in m], 6,
        )
        res = [res[a] + (flux[a] - pltpu.roll(flux[a], 1, 1)) for a in range(3)]
        back = pltpu.roll(coupling, 1, 1)
        cyu[k] = coupling
        cyd[k] = back
        inv[k] = st + (coupling + back)
        for a in range(3):
            res_ref[a, k] = res[a]
        if k > 0:
            flux, coupling = face(
                p_ref[k - 1], mobilities(s_ref[0, k - 1], s_ref[1, k - 1]), tr_ref[0, k - 1],
                bits_ref[k - 1], p, m, 0,
            )
            cz[k] = coupling
            inv[k] += coupling
            inv[k - 1] += coupling
            for a in range(3):
                res_ref[a, k] -= flux[a]
                res_ref[a, k - 1] += flux[a]

    for c in halo_copies:
        c.wait_recv()

    p = p_ref[0]
    m = mobilities(s_ref[0, 0], s_ref[1, 0])
    flux, coupling = face(
        halo_lo[0], mobilities(halo_lo[1], halo_lo[2]), halo_lo[3] * not_first_slab,
        halo_lo[4].astype(jnp.int32), p, m, 0,
    )
    cz[0] = coupling
    inv[0] += coupling
    for a in range(3):
        res_ref[a, 0] -= flux[a]
    p = p_ref[top]
    m = mobilities(s_ref[0, top], s_ref[1, top])
    flux, coupling = face(
        p, m, tr_ref[0, top] * not_last_slab, bits_ref[top],
        halo_hi[0], mobilities(halo_hi[1], halo_hi[2]), 0,
    )
    cz[LAYERS] = coupling
    inv[top] += coupling
    for a in range(3):
        res_ref[a, top] += flux[a]

    first_p = rdn_stage[0]
    low_flux, low_link = face(
        rhalo_lo[0], mobilities(rhalo_lo[1], rhalo_lo[2]), rhalo_lo[3] * not_first_sector,
        rhalo_lo[4].astype(jnp.int32), first_p, mobilities(rdn_stage[1], rdn_stage[2]), 3,
    )
    hi_m = mobilities(rhalo_hi[1], rhalo_hi[2])
    for k in range(LAYERS):
        p = p_ref[k]
        m = mobilities(s_ref[0, k], s_ref[1, k])

        def after(x, edge):
            return jnp.where(row2 == last, edge[k : k + 1], pltpu.roll(x, last, 0))

        def before(x, edge):
            return jnp.where(row2 == 0, edge[k : k + 1], pltpu.roll(x, 1, 0))

        weight = tr_ref[1, k] * jnp.where(row2 == last, not_last_sector, 1.0)
        flux, coupling = face(
            p, m, weight, bits_ref[k], after(p, rhalo_hi[0]),
            [after(m[a], hi_m[a]) for a in range(3)], 3,
        )
        back = before(coupling, low_link)
        cxu[k] = coupling
        cxd[k] = back
        inv[k] += coupling + back
        for a in range(3):
            res_ref[a, k] += flux[a] - before(flux[a], low_flux[a])

    zero_tile = jnp.zeros((CHUNKS, 128), F32)
    layer_source = [zero_tile] * LAYERS
    for d in range(others):
        fault_copy(others - 1 - d).wait_recv()
        flags = fup[d]
        w = fweight[d]
        flux, coupling = face(
            own[d, 0], mobilities(own[d, 1], own[d, 2]), w, flags,
            far[d, 0], mobilities(far[d, 1], far[d, 2]), 0,
        )
        for a in range(3):
            vals[d, a] = flux[a]
        vals[d, 3] = coupling
        link[d] = coupling
        layer = jnp.right_shift(cell[d], 13)
        total = flux[0] + flux[1] + flux[2]
        for k in range(LAYERS):
            layer_source[k] = layer_source[k] - jnp.where(layer == k, total, 0.0)

    for k in range(LAYERS):
        regular = -(res_ref[0, k] + res_ref[1, k] + res_ref[2, k])
        source = jnp.sum(regular, axis=0, keepdims=True) + jnp.sum(
            layer_source[k], axis=0, keepdims=True
        )
        asend[k : k + 1, :] = jnp.sum(storage[k], axis=0, keepdims=True)
        asend[4 + k : 5 + k, :] = jnp.sum(cz[k + 1], axis=0, keepdims=True)
        asend[8 + k : 9 + k, :] = source
    asend[12:16, :] = jnp.zeros((4, 128), F32)

    def a_copy(d):
        return copy(asend, arecv.at[others - 1 - d], a_ss.at[d], a_rs.at[others - 1 - d],
                    (sector_of(d + 1), t))

    @pl.loop(0, others)
    def _(d):
        a_copy(d).start()

    def masked(d, field, count):
        pieces = []
        for b in range(CHUNKS):
            value = field[b : b + 1, :]
            mask = ohlo[d, :, b * 128 : (b + 1) * 128]
            pieces.append(jnp.concatenate([mask * x for x in split(value, count)], 0))
        return jnp.concatenate(pieces, 1)

    nt = (((1,), (1,)), ((), ()))
    acc[...] = jnp.zeros(acc.shape, F32)

    @pl.loop(0, others)
    def _(d):
        for i in range(4):
            acc[i] += lax.dot_general(
                masked(d, vals.at[d, i], 3), oh[d], nt, preferred_element_type=F32
            )

    def unfold(total):
        return total.T.reshape(LAYERS, ROWS, COLS)

    for i in range(4):
        placed = unfold(acc[i, :128] + (acc[i, 128:256] + acc[i, 256:]))
        if i < 3:
            res_ref[i] += placed
        else:
            inv[...] = RELAXATION / (inv[...] + placed)
    for k in range(LAYERS):
        rhs[k] = -(res_ref[0, k] + res_ref[1, k] + res_ref[2, k])

    sums = asend[...]
    for d in range(others):
        a_copy(others - 1 - d).wait_recv()
        sums = sums + arecv[d]
    column = jnp.sum(sums, axis=1, keepdims=True)
    lane16 = lax.broadcasted_iota(jnp.int32, (16, 128), 1)
    row16 = lax.broadcasted_iota(jnp.int32, (16, 128), 0)
    spread = jnp.where(
        jnp.bitwise_and(lane16, 3) == jnp.bitwise_and(row16, 3), jnp.broadcast_to(column, (16, 128)), 0.0
    )
    for q in range(4):
        bsend[q : q + 1, :] = jnp.sum(spread[4 * q : 4 * q + 4], axis=0, keepdims=True)
    brecv[t] = bsend[...]

    def b_copy(k, dst):
        return copy(bsend, brecv.at[dst], b_ss.at[k - 1], b_rs.at[k - 1],
                    (me, lax.rem(t + k, n_slab)))

    @pl.loop(1, n_slab)
    def _(k):
        b_copy(k, t).start()

    @pl.loop(1, n_slab)
    def _(k):
        b_copy(k, lax.rem(t + n_slab - k, n_slab)).wait_recv()

    lane4 = lax.broadcasted_iota(jnp.int32, (4, 128), 1)
    rows = jnp.zeros((4, 128), F32)
    for j in range(n_slab):
        rows = rows + jnp.where(jnp.right_shift(lane4, 2) == j, brecv[j], 0.0)
    s_row, right, rhs_row = rows[0:1], rows[1:2], rows[2:3]
    lane1 = lax.broadcasted_iota(jnp.int32, (1, 128), 1)
    right = jnp.where(lane1 < LAYERS * n_slab - 1, right, 0.0)
    s_row = jnp.where(lane1 < LAYERS * n_slab, s_row, 1.0)
    left = jnp.where(lane1 > 0, pltpu.roll(right, 1, 1), 0.0)
    step = 1
    while step < LAYERS * n_slab:
        pivot = 1.0 / (s_row + left + right)
        sn, ln, rn, dn = s_row * pivot, left * pivot, right * pivot, rhs_row * pivot
        s_row = s_row + left * pltpu.roll(sn, step, 1) + right * pltpu.roll(sn, 128 - step, 1)
        rhs_row = rhs_row + left * pltpu.roll(dn, step, 1) + right * pltpu.roll(dn, 128 - step, 1)
        left = left * pltpu.roll(ln, step, 1)
        right = right * pltpu.roll(rn, 128 - step, 1)
        step *= 2
    coarse = rhs_row / s_row
    lane8 = lax.broadcasted_iota(jnp.int32, (8, 128), 1)
    row8 = lax.broadcasted_iota(jnp.int32, (8, 128), 0)
    level = jnp.sum(
        jnp.where(lane8 == row8 + (LAYERS * t - 1), jnp.broadcast_to(coarse, (8, 128)), 0.0),
        axis=1, keepdims=True,
    )
    level = jnp.broadcast_to(level, (8, 128))

    def level_row(k):
        return level[k + 1 : k + 2]

    def fault_extra(value_of):
        def body(d, total):
            vals[d, 0] = link[d] * value_of(d)
            return total + lax.dot_general(
                masked(d, vals.at[d, 0], 2), oh[d], nt, preferred_element_type=F32
            )

        total = lax.fori_loop(0, others, body, jnp.zeros((256, 256), F32))
        return unfold(total[:128] + total[128:])

    def coarse_far(d):
        value = zero_tile
        for k in range(LAYERS):
            value = jnp.where(far[d, 3] == k, level_row(k), value)
        return value

    part[...] = fault_extra(coarse_far)
    for k in range(LAYERS):
        here = level_row(k)
        total = part[k] + rhs[k] + cz[k + 1] * level_row(k + 1) + cz[k] * level_row(k - 1)
        total = total + (cxu[k] + cxd[k] + cyu[k] + cyd[k]) * here
        ubuf[k] = (1.0 - RELAXATION) * here + inv[k] * total

    sends = []
    for sweep in range(SWEEPS - 1):
        for k in range(LAYERS):
            xup[sweep, k : k + 1, :] = ubuf[k, last:]
            xdn[sweep, k : k + 1, :] = ubuf[k, :1]
        usend[sweep, 0] = ubuf[top]
        usend[sweep, 1] = ubuf[0]
        edge_copies = [
            copy(usend.at[sweep, 0], zlo.at[sweep], w_ss.at[sweep, 0], w_rs.at[sweep, 0], (me, t_next)),
            copy(usend.at[sweep, 1], zhi.at[sweep], w_ss.at[sweep, 1], w_rs.at[sweep, 1], (me, t_prev)),
            copy(xup.at[sweep], xlo.at[sweep], w_ss.at[sweep, 2], w_rs.at[sweep, 2], (s_next, t)),
            copy(xdn.at[sweep], xhi.at[sweep], w_ss.at[sweep, 3], w_rs.at[sweep, 3], (s_prev, t)),
        ]
        for c in edge_copies:
            c.start()
        sends += edge_copies
        flipped = ubuf[...].reshape(CELLS_HI, COLS).T
        weights = jnp.concatenate(split(flipped, 2), 0)
        fsplit[0, :256, :] = weights

        def u_copy(d, sweep=sweep):
            return copy(
                uown.at[sweep, d], urecv.at[sweep, others - 1 - d],
                u_ss.at[sweep, d], u_rs.at[sweep, others - 1 - d], (sector_of(d + 1), t),
            )

        @pl.loop(0, others)
        def _(d, sweep=sweep, u_copy=u_copy):
            def store(i, b, row):
                uown[sweep, d, pl.ds(b, 1), :] = row

            gather(d, [fsplit[0, :256]], 2, store)
            u_copy(d).start()

        for k in range(LAYERS):
            u = ubuf[k]
            total = rhs[k] + cyu[k] * pltpu.roll(u, COLS - 1, 1) + cyd[k] * pltpu.roll(u, 1, 1)
            total = total + cxu[k] * jnp.where(row2 == last, 0.0, pltpu.roll(u, last, 0))
            total = total + cxd[k] * jnp.where(row2 == 0, 0.0, pltpu.roll(u, 1, 0))
            if k > 0:
                total = total + cz[k] * ubuf[k - 1]
            if k < top:
                total = total + cz[k + 1] * ubuf[k + 1]
            part[k] = total
        for c in edge_copies:
            c.wait_recv()
        part[0] += cz[0] * zlo[sweep]
        part[top] += cz[LAYERS] * zhi[sweep]
        for k in range(LAYERS):
            part[k, last:] += cxu[k, last:] * xhi[sweep, k : k + 1, :]
            part[k, :1] += cxd[k, :1] * xlo[sweep, k : k + 1, :]
        for d in range(others):
            u_copy(others - 1 - d).wait_recv()
        target = out_ref if sweep == SWEEPS - 2 else ubuf
        extra = fault_extra(lambda d, sweep=sweep: urecv[sweep, d])
        for k in range(LAYERS):
            target[k] = (1.0 - RELAXATION) * ubuf[k] + inv[k] * (part[k] + extra[k])

    for c in halo_copies + sends:
        c.wait_send()
    for d in range(others):
        fault_copy(d).wait_send()
        a_copy(d).wait_send()
        for sweep in range(SWEEPS - 1):
            copy(
                uown.at[sweep, d], urecv.at[sweep, others - 1 - d],
                u_ss.at[sweep, d], u_rs.at[sweep, others - 1 - d], (sector_of(d + 1), t),
            ).wait_send()

    @pl.loop(1, n_slab)
    def _(k):
        b_copy(k, t).wait_send()


def body(n_sector, n_slab, *args):
    vmem = pl.BlockSpec(memory_space=pltpu.VMEM)
    smem = pl.BlockSpec(memory_space=pltpu.SMEM)
    others = n_sector - 1
    rounds = SWEEPS - 1
    block = (LAYERS, ROWS, COLS)
    tiles = (CHUNKS, 128)

    def f32(*shape):
        return pltpu.VMEM(shape, F32)

    def i32(*shape):
        return pltpu.VMEM(shape, jnp.int32)

    def sem(*shape):
        return pltpu.SemaphoreType.DMA(shape)

    scratch = dict(
        oh=pltpu.VMEM((others, CELLS_HI, SLOTS), BF),
        ohlo=pltpu.VMEM((others, 128, SLOTS), BF),
        fsplit=pltpu.VMEM((3, 384, CELLS_HI), BF),
        acc=f32(4, 384, CELLS_HI),
        cell=i32(others, *tiles),
        fweight=f32(others, *tiles),
        fup=i32(others, *tiles),
        own=f32(others, 4, *tiles),
        far=f32(others, 4, *tiles),
        link=f32(others, *tiles),
        vals=f32(others, 4, *tiles),
        up_stage=f32(5, ROWS, COLS),
        dn_stage=f32(3, ROWS, COLS),
        halo_lo=f32(5, ROWS, COLS),
        halo_hi=f32(3, ROWS, COLS),
        rup_stage=f32(5, LAYERS, COLS),
        rdn_stage=f32(3, LAYERS, COLS),
        rhalo_lo=f32(5, LAYERS, COLS),
        rhalo_hi=f32(3, LAYERS, COLS),
        asend=f32(16, 128),
        arecv=f32(others, 16, 128),
        bsend=f32(4, 128),
        brecv=f32(n_slab, 4, 128),
        cz=f32(LAYERS + 1, ROWS, COLS),
        cxu=f32(*block),
        cxd=f32(*block),
        cyu=f32(*block),
        cyd=f32(*block),
        storage=f32(*block),
        rhs=f32(*block),
        inv=f32(*block),
        ubuf=f32(*block),
        part=f32(*block),
        uown=f32(rounds, others, *tiles),
        urecv=f32(rounds, others, *tiles),
        usend=f32(rounds, 2, ROWS, COLS),
        zlo=f32(rounds, ROWS, COLS),
        zhi=f32(rounds, ROWS, COLS),
        xup=f32(rounds, LAYERS, COLS),
        xdn=f32(rounds, LAYERS, COLS),
        xlo=f32(rounds, LAYERS, COLS),
        xhi=f32(rounds, LAYERS, COLS),
        f_ss=sem(others), f_rs=sem(others),
        h_ss=sem(4), h_rs=sem(4),
        a_ss=sem(others), a_rs=sem(others),
        b_ss=sem(n_slab - 1), b_rs=sem(n_slab - 1),
        u_ss=sem(rounds, others), u_rs=sem(rounds, others),
        w_ss=sem(rounds, 4), w_rs=sem(rounds, 4),
    )
    names = list(scratch)

    def run(*refs):
        kernel(n_sector, n_slab, *refs[:12], **dict(zip(names, refs[12:])))

    in_specs = [vmem] * 10
    in_specs[7] = smem
    return pl.pallas_call(
        run,
        out_shape=(
            jax.ShapeDtypeStruct((3, *block), F32),
            jax.ShapeDtypeStruct(block, F32),
        ),
        in_specs=in_specs,
        out_specs=(vmem, vmem),
        scratch_shapes=list(scratch.values()),
        compiler_params=pltpu.CompilerParams(
            collective_id=0, has_side_effects=True, vmem_limit_bytes=48 * 2**20
        ),
    )(*args)


def solution(mesh):
    placed = (
        P("slab", "sector", None),
        P(None, "slab", "sector", None),
        P(None, "slab", "sector", None),
        P("slab", "sector", None),
        P(None, "slab", "sector", None),
        P("slab", "sector", None),
        P("slab", "sector", None, None),
        P("slab", "sector", None),
        P("slab", "sector", None, None),
        P("slab", "sector", None, None),
    )
    return jax.shard_map(
        functools.partial(body, mesh.shape["sector"], mesh.shape["slab"]),
        mesh=mesh,
        in_specs=placed,
        out_specs=(P(None, "slab", "sector", None), P("slab", "sector", None)),
        check_vma=False,
    )
```

```python
import functools

import jax
import jax.numpy as jnp
from jax import lax
from jax.experimental import pallas as pl
from jax.experimental.pallas import tpu as pltpu
from jax.sharding import PartitionSpec as P

COMPRESS = (0.0002, 0.0005, 0.002)
VISCOSITY = (1.0, 3.0, 0.5)
RELAXATION = 2.0 / 3.0
SWEEPS = 4

BF = jnp.bfloat16
F32 = jnp.float32
MESH = pl.DeviceIdType.MESH

LAYERS, ROWS, COLS = 4, 64, 128
CELLS_HI = LAYERS * ROWS
SLOTS = 1024
CHUNKS = SLOTS // 128


def split(value, count):
    parts = []
    for _ in range(count - 1):
        part = value.astype(BF)
        parts.append(part)
        value = value - part.astype(F32)
    parts.append(value.astype(BF))
    return parts


def mobilities(s_water, s_gas):
    s_oil = 1.0 - s_water - s_gas
    return [s * s * (1.0 / v) for s, v in zip((s_water, s_oil, s_gas), VISCOSITY)]


def face(p_low, m_low, weight, words, p_high, m_high, first_bit):
    drop = p_low - p_high
    fluxes, total = [], None
    for a in range(3):
        flag = jnp.bitwise_and(words, 1 << (first_bit + a)) != 0
        part = weight * jnp.where(flag, m_low[a], m_high[a])
        fluxes.append(part * drop)
        total = part if total is None else total + part
    return fluxes, total


def kernel(
    n_sector, n_slab,
    inputs, res_ref, out_ref, *,
    p_ref, s_ref, om_ref, pv_ref, tr_ref, bits_ref, fc_ref, cnt_ref, ft_ref, fu_ref, in_sem,
    oh, ohlo, fsplit, cell, fweight, fup, own, far, link, vals,
    up_stage, dn_stage, halo_lo, halo_hi, rup_stage, rdn_stage, rhalo_lo, rhalo_hi,
    asend, arecv, bsend, brecv,
    cz, cxu, cxd, cyu, cyd, storage, rhs, inv, ubuf, part,
    uown, urecv, usend, zlo, zhi, xup, xdn, xlo, xhi,
    f_ss, f_rs, h_ss, h_rs, a_ss, a_rs, b_ss, b_rs, u_ss, u_rs, w_ss, w_rs,
):
    me = lax.axis_index("sector")
    t = lax.axis_index("slab")
    others = n_sector - 1
    s_next = lax.rem(me + 1, n_sector)
    s_prev = lax.rem(me + n_sector - 1, n_sector)
    t_next = lax.rem(t + 1, n_slab)
    t_prev = lax.rem(t + n_slab - 1, n_slab)

    def copy(src, dst, ss, rs, device):
        return pltpu.make_async_remote_copy(
            src_ref=src, dst_ref=dst, send_sem=ss, recv_sem=rs,
            device_id=device, device_id_type=MESH,
        )

    far_first = sorted(range(others), key=lambda d: (-min(d + 1, n_sector - d - 1), d))
    arrivals = [others - 1 - d for d in far_first]

    def sector_of(d):
        return lax.rem(me + d, n_sector)

    held = (p_ref, s_ref, om_ref, pv_ref, tr_ref, bits_ref, fc_ref, cnt_ref, ft_ref, fu_ref)
    loads = [
        pltpu.make_async_copy(src, dst, in_sem.at[i])
        for i, (src, dst) in enumerate(zip(inputs, held))
    ]
    for i in (6, 7, 8, 9, 0, 1, 4, 5, 3, 2):
        loads[i].start()
    barrier = pltpu.get_barrier_semaphore()

    @pl.loop(1, n_sector)
    def _(d):
        pl.semaphore_signal(barrier, inc=1, device_id=(sector_of(d), t), device_id_type=MESH)

    @pl.loop(1, n_slab)
    def _(k):
        pl.semaphore_signal(
            barrier, inc=1, device_id=(me, lax.rem(t + k, n_slab)), device_id_type=MESH
        )

    for i in (6, 7, 8, 9, 0, 1, 4, 5):
        loads[i].wait()
    top = LAYERS - 1
    for i, plane in enumerate((p_ref[top], s_ref[0, top], s_ref[1, top], tr_ref[0, top])):
        up_stage[i] = plane
    up_stage[4] = bits_ref[top].astype(F32)
    for i, plane in enumerate((p_ref[0], s_ref[0, 0], s_ref[1, 0])):
        dn_stage[i] = plane
    last = ROWS - 1
    for k in range(LAYERS):
        for i, row in enumerate(
            (p_ref[k, last:], s_ref[0, k, last:], s_ref[1, k, last:], tr_ref[1, k, last:])
        ):
            rup_stage[i, k : k + 1, :] = row
        rup_stage[4, k : k + 1, :] = bits_ref[k, last:].astype(F32)
        for i, row in enumerate((p_ref[k, :1], s_ref[0, k, :1], s_ref[1, k, :1])):
            rdn_stage[i, k : k + 1, :] = row

    lane = lax.broadcasted_iota(jnp.int32, (1, 128), 1)
    counts = [cnt_ref[0, 0, sector_of(d)] for d in range(1, n_sector)]
    turn = lax.rem(n_sector - me, n_sector)
    for b in range(CHUNKS):
        span = slice(b * 128, (b + 1) * 128)
        cells = pltpu.roll(fc_ref[0, 0, :, span], turn, 0)
        flags = pltpu.roll(fu_ref[0, 0, :, span], turn, 0)
        trans = pltpu.roll(ft_ref[0, 0, :, span], turn, 0)
        for d in range(others):
            row = slice(d + 1, d + 2)
            cell[d, b : b + 1, :] = cells[row]
            fup[d, b : b + 1, :] = flags[row]
            fweight[d, b : b + 1, :] = jnp.where(lane + b * 128 < counts[d], trans[row], 0.0)

    for i, field in enumerate((p_ref, s_ref.at[0], s_ref.at[1])):
        flipped = field[...].reshape(CELLS_HI, COLS).T
        for j, piece in enumerate(split(flipped, 3)):
            fsplit[i, j * 128 : (j + 1) * 128, :] = piece

    sub = lax.broadcasted_iota(jnp.int32, (128, 128), 0)
    sub_hi = lax.broadcasted_iota(jnp.int32, (CELLS_HI, 128), 0)

    @pl.loop(0, others)
    def _(d):
        for b in range(CHUNKS):
            span = slice(b * 128, (b + 1) * 128)
            c = cell[d, b : b + 1, :]
            oh[d, :, span] = jnp.where(sub_hi == jnp.right_shift(c, 7), 1.0, 0.0).astype(BF)
            ohlo[d, :, span] = jnp.where(sub == jnp.bitwise_and(c, 127), 1.0, 0.0).astype(BF)

    pl.semaphore_wait(barrier, n_sector - 1 + n_slab - 1)

    halo_copies = [
        copy(up_stage, halo_lo, h_ss.at[0], h_rs.at[0], (me, t_next)),
        copy(dn_stage, halo_hi, h_ss.at[1], h_rs.at[1], (me, t_prev)),
        copy(rup_stage, rhalo_lo, h_ss.at[2], h_rs.at[2], (s_next, t)),
        copy(rdn_stage, rhalo_hi, h_ss.at[3], h_rs.at[3], (s_prev, t)),
    ]
    for c in halo_copies:
        c.start()

    def gather(d, weights, count, store):
        rows = [jnp.bitwise_and(cell[d, b : b + 1, :], 127) for b in range(CHUNKS)]
        for i, w in enumerate(weights):
            for b in range(CHUNKS // 2):
                picks = oh[d, :, b * 256 : (b + 1) * 256]
                g = jnp.dot(w, picks, preferred_element_type=F32)
                total = g[(count - 1) * 128 :]
                for j in reversed(range(count - 1)):
                    total = g[j * 128 : (j + 1) * 128] + total
                for k in range(2):
                    found = jnp.where(
                        sub == rows[2 * b + k], total[:, k * 128 : (k + 1) * 128], 0.0
                    )
                    store(i, 2 * b + k, jnp.sum(found, axis=0, keepdims=True))

    def fault_copy(d):
        return copy(own.at[d], far.at[others - 1 - d], f_ss.at[d], f_rs.at[others - 1 - d],
                    (sector_of(d + 1), t))

    for d in far_first:

        def store(i, b, row, d=d):
            own[d, i, b : b + 1, :] = row

        gather(d, [fsplit[i] for i in range(3)], 3, store)
        own[d, 3] = jnp.right_shift(cell[d], 13).astype(F32)
        fault_copy(d).start()

    lane2 = lax.broadcasted_iota(jnp.int32, (ROWS, COLS), 1)
    row2 = lax.broadcasted_iota(jnp.int32, (ROWS, COLS), 0)
    not_first_slab = jnp.where(t > 0, 1.0, 0.0).astype(F32)
    not_last_slab = jnp.where(t < n_slab - 1, 1.0, 0.0).astype(F32)
    not_first_sector = jnp.where(me > 0, 1.0, 0.0).astype(F32)
    not_last_sector = jnp.where(me < n_sector - 1, 1.0, 0.0).astype(F32)

    loads[3].wait()
    loads[2].wait()
    for k in range(LAYERS):
        p = p_ref[k]
        pv = pv_ref[k]
        sw, sg = s_ref[0, k], s_ref[1, k]
        so = 1.0 - sw - sg
        m = mobilities(sw, sg)
        words = bits_ref[k]
        sat = (sw, so, sg)
        st = pv * (sw * COMPRESS[0] + so * COMPRESS[1] + sg * COMPRESS[2])
        storage[k] = st
        res = [pv * sat[a] * (1.0 + COMPRESS[a] * p) - om_ref[a, k] for a in range(3)]
        flux, coupling = face(
            p, m, jnp.where(lane2 < COLS - 1, tr_ref[2, k], 0.0), words,
            pltpu.roll(p, COLS - 1, 1), [pltpu.roll(x, COLS - 1, 1) for x in m], 6,
        )
        res = [res[a] + (flux[a] - pltpu.roll(flux[a], 1, 1)) for a in range(3)]
        back = pltpu.roll(coupling, 1, 1)
        cyu[k] = coupling
        cyd[k] = back
        inv[k] = st + (coupling + back)
        for a in range(3):
            res_ref[a, k] = res[a]
        if k > 0:
            flux, coupling = face(
                p_ref[k - 1], mobilities(s_ref[0, k - 1], s_ref[1, k - 1]), tr_ref[0, k - 1],
                bits_ref[k - 1], p, m, 0,
            )
            cz[k] = coupling
            inv[k] += coupling
            inv[k - 1] += coupling
            for a in range(3):
                res_ref[a, k] -= flux[a]
                res_ref[a, k - 1] += flux[a]

    for c in halo_copies:
        c.wait_recv()

    p = p_ref[0]
    m = mobilities(s_ref[0, 0], s_ref[1, 0])
    flux, coupling = face(
        halo_lo[0], mobilities(halo_lo[1], halo_lo[2]), halo_lo[3] * not_first_slab,
        halo_lo[4].astype(jnp.int32), p, m, 0,
    )
    cz[0] = coupling
    inv[0] += coupling
    for a in range(3):
        res_ref[a, 0] -= flux[a]
    p = p_ref[top]
    m = mobilities(s_ref[0, top], s_ref[1, top])
    flux, coupling = face(
        p, m, tr_ref[0, top] * not_last_slab, bits_ref[top],
        halo_hi[0], mobilities(halo_hi[1], halo_hi[2]), 0,
    )
    cz[LAYERS] = coupling
    inv[top] += coupling
    for a in range(3):
        res_ref[a, top] += flux[a]

    first_p = rdn_stage[0]
    low_flux, low_link = face(
        rhalo_lo[0], mobilities(rhalo_lo[1], rhalo_lo[2]), rhalo_lo[3] * not_first_sector,
        rhalo_lo[4].astype(jnp.int32), first_p, mobilities(rdn_stage[1], rdn_stage[2]), 3,
    )
    hi_m = mobilities(rhalo_hi[1], rhalo_hi[2])
    for k in range(LAYERS):
        p = p_ref[k]
        m = mobilities(s_ref[0, k], s_ref[1, k])

        def after(x, edge):
            return jnp.where(row2 == last, edge[k : k + 1], pltpu.roll(x, last, 0))

        def before(x, edge):
            return jnp.where(row2 == 0, edge[k : k + 1], pltpu.roll(x, 1, 0))

        weight = tr_ref[1, k] * jnp.where(row2 == last, not_last_sector, 1.0)
        flux, coupling = face(
            p, m, weight, bits_ref[k], after(p, rhalo_hi[0]),
            [after(m[a], hi_m[a]) for a in range(3)], 3,
        )
        back = before(coupling, low_link)
        cxu[k] = coupling
        cxd[k] = back
        inv[k] += coupling + back
        for a in range(3):
            res_ref[a, k] += flux[a] - before(flux[a], low_flux[a])

    zero_tile = jnp.zeros((CHUNKS, 128), F32)
    layer_source = [zero_tile] * LAYERS
    for d in arrivals:
        fault_copy(others - 1 - d).wait_recv()
        flags = fup[d]
        w = fweight[d]
        flux, coupling = face(
            own[d, 0], mobilities(own[d, 1], own[d, 2]), w, flags,
            far[d, 0], mobilities(far[d, 1], far[d, 2]), 0,
        )
        for a in range(3):
            vals[d, a] = flux[a]
        vals[d, 3] = coupling
        link[d] = coupling
        layer = jnp.right_shift(cell[d], 13)
        total = flux[0] + flux[1] + flux[2]
        for k in range(LAYERS):
            layer_source[k] = layer_source[k] - jnp.where(layer == k, total, 0.0)

    for k in range(LAYERS):
        regular = -(res_ref[0, k] + res_ref[1, k] + res_ref[2, k])
        source = jnp.sum(regular, axis=0, keepdims=True) + jnp.sum(
            layer_source[k], axis=0, keepdims=True
        )
        asend[k : k + 1, :] = jnp.sum(storage[k], axis=0, keepdims=True)
        asend[4 + k : 5 + k, :] = jnp.sum(cz[k + 1], axis=0, keepdims=True)
        asend[8 + k : 9 + k, :] = source
    asend[12:16, :] = jnp.zeros((4, 128), F32)

    def a_copy(d):
        return copy(asend, arecv.at[others - 1 - d], a_ss.at[d], a_rs.at[others - 1 - d],
                    (sector_of(d + 1), t))

    @pl.loop(0, others)
    def _(d):
        a_copy(d).start()

    nt = (((1,), (1,)), ((), ()))

    def masked(d, field):
        pieces = []
        for b in range(CHUNKS):
            mask = ohlo[d, :, b * 128 : (b + 1) * 128]
            parts = split(field[b : b + 1, :], 2)
            pieces.append(jnp.concatenate([mask * x for x in parts], 0))
        return jnp.concatenate(pieces, 1)

    def scatter(fields):
        total = None
        for d in range(others):
            rows = jnp.concatenate([masked(d, vals.at[d, i]) for i in fields], 0)
            part = lax.dot_general(rows, oh[d], nt, preferred_element_type=F32)
            total = part if total is None else total + part
        return [
            (total[256 * i : 256 * i + 128] + total[256 * i + 128 : 256 * i + 256])
            .T.reshape(LAYERS, ROWS, COLS)
            for i in range(len(fields))
        ]

    placed = scatter((0, 1))
    res_ref[0] += placed[0]
    res_ref[1] += placed[1]

    sums = asend[...]
    for d in range(others):
        a_copy(others - 1 - d).wait_recv()
        sums = sums + arecv[d]
    column = jnp.sum(sums, axis=1, keepdims=True)
    lane16 = lax.broadcasted_iota(jnp.int32, (16, 128), 1)
    row16 = lax.broadcasted_iota(jnp.int32, (16, 128), 0)
    spread = jnp.where(
        jnp.bitwise_and(lane16, 3) == jnp.bitwise_and(row16, 3),
        jnp.broadcast_to(column, (16, 128)), 0.0,
    )
    for q in range(4):
        bsend[q : q + 1, :] = jnp.sum(spread[4 * q : 4 * q + 4], axis=0, keepdims=True)
    brecv[t] = bsend[...]

    def b_copy(k, dst):
        return copy(bsend, brecv.at[dst], b_ss.at[k - 1], b_rs.at[k - 1],
                    (me, lax.rem(t + k, n_slab)))

    @pl.loop(1, n_slab)
    def _(k):
        b_copy(k, t).start()

    placed = scatter((2, 3))
    res_ref[2] += placed[0]
    inv[...] = RELAXATION / (inv[...] + placed[1])
    for k in range(LAYERS):
        rhs[k] = -(res_ref[0, k] + res_ref[1, k] + res_ref[2, k])

    @pl.loop(1, n_slab)
    def _(k):
        b_copy(k, lax.rem(t + n_slab - k, n_slab)).wait_recv()

    lane4 = lax.broadcasted_iota(jnp.int32, (4, 128), 1)
    rows = jnp.zeros((4, 128), F32)
    for j in range(n_slab):
        rows = rows + jnp.where(jnp.right_shift(lane4, 2) == j, brecv[j], 0.0)
    s_row, right, rhs_row = rows[0:1], rows[1:2], rows[2:3]
    lane1 = lax.broadcasted_iota(jnp.int32, (1, 128), 1)
    right = jnp.where(lane1 < LAYERS * n_slab - 1, right, 0.0)
    s_row = jnp.where(lane1 < LAYERS * n_slab, s_row, 1.0)
    left = jnp.where(lane1 > 0, pltpu.roll(right, 1, 1), 0.0)
    step = 1
    while step < LAYERS * n_slab:
        pivot = 1.0 / (s_row + left + right)
        sn, ln, rn, dn = s_row * pivot, left * pivot, right * pivot, rhs_row * pivot
        s_row = s_row + left * pltpu.roll(sn, step, 1) + right * pltpu.roll(sn, 128 - step, 1)
        rhs_row = rhs_row + left * pltpu.roll(dn, step, 1) + right * pltpu.roll(dn, 128 - step, 1)
        left = left * pltpu.roll(ln, step, 1)
        right = right * pltpu.roll(rn, 128 - step, 1)
        step *= 2
    coarse = rhs_row / s_row
    lane8 = lax.broadcasted_iota(jnp.int32, (8, 128), 1)
    row8 = lax.broadcasted_iota(jnp.int32, (8, 128), 0)
    level = jnp.sum(
        jnp.where(lane8 == row8 + (LAYERS * t - 1), jnp.broadcast_to(coarse, (8, 128)), 0.0),
        axis=1, keepdims=True,
    )
    level = jnp.broadcast_to(level, (8, 128))

    def level_row(k):
        return level[k + 1 : k + 2]

    def fault_extra(order, value_of):
        total = None
        for d in order:
            vals[d, 0] = link[d] * value_of(d)
            part = lax.dot_general(
                oh[d], masked(d, vals.at[d, 0]), nt, preferred_element_type=F32
            )
            total = part if total is None else total + part
        return (total[:, :128] + total[:, 128:]).reshape(LAYERS, ROWS, COLS)

    def coarse_far(d):
        value = zero_tile
        for k in range(LAYERS):
            value = jnp.where(far[d, 3] == k, level_row(k), value)
        return value

    part[...] = fault_extra(range(others), coarse_far)
    for k in range(LAYERS):
        here = level_row(k)
        total = part[k] + rhs[k] + cz[k + 1] * level_row(k + 1) + cz[k] * level_row(k - 1)
        total = total + (cxu[k] + cxd[k] + cyu[k] + cyd[k]) * here
        ubuf[k] = (1.0 - RELAXATION) * here + inv[k] * total

    sends = []
    for sweep in range(SWEEPS - 1):
        for k in range(LAYERS):
            xup[sweep, k : k + 1, :] = ubuf[k, last:]
            xdn[sweep, k : k + 1, :] = ubuf[k, :1]
        usend[sweep, 0] = ubuf[top]
        usend[sweep, 1] = ubuf[0]
        edge_copies = [
            copy(usend.at[sweep, 0], zlo.at[sweep], w_ss.at[sweep, 0], w_rs.at[sweep, 0], (me, t_next)),
            copy(usend.at[sweep, 1], zhi.at[sweep], w_ss.at[sweep, 1], w_rs.at[sweep, 1], (me, t_prev)),
            copy(xup.at[sweep], xlo.at[sweep], w_ss.at[sweep, 2], w_rs.at[sweep, 2], (s_next, t)),
            copy(xdn.at[sweep], xhi.at[sweep], w_ss.at[sweep, 3], w_rs.at[sweep, 3], (s_prev, t)),
        ]
        for c in edge_copies:
            c.start()
        sends += edge_copies
        flipped = ubuf[...].reshape(CELLS_HI, COLS).T
        weights = jnp.concatenate(split(flipped, 2), 0)
        fsplit[0, :256, :] = weights

        def u_copy(d, sweep=sweep):
            return copy(
                uown.at[sweep, d], urecv.at[sweep, others - 1 - d],
                u_ss.at[sweep, d], u_rs.at[sweep, others - 1 - d], (sector_of(d + 1), t),
            )

        weights = fsplit[0, :256]
        for d in far_first:

            def store(i, b, row, d=d):
                uown[sweep, d, b : b + 1, :] = row

            gather(d, [weights], 2, store)
            u_copy(d).start()

        for k in range(LAYERS):
            u = ubuf[k]
            total = rhs[k] + cyu[k] * pltpu.roll(u, COLS - 1, 1) + cyd[k] * pltpu.roll(u, 1, 1)
            total = total + cxu[k] * jnp.where(row2 == last, 0.0, pltpu.roll(u, last, 0))
            total = total + cxd[k] * jnp.where(row2 == 0, 0.0, pltpu.roll(u, 1, 0))
            if k > 0:
                total = total + cz[k] * ubuf[k - 1]
            if k < top:
                total = total + cz[k + 1] * ubuf[k + 1]
            part[k] = total

        def arrived(d, sweep=sweep, u_copy=u_copy):
            u_copy(others - 1 - d).wait_recv()
            return urecv[sweep, d]

        extra = fault_extra(arrivals, arrived)
        for c in edge_copies:
            c.wait_recv()
        part[0] += cz[0] * zlo[sweep]
        part[top] += cz[LAYERS] * zhi[sweep]
        for k in range(LAYERS):
            part[k, last:] += cxu[k, last:] * xhi[sweep, k : k + 1, :]
            part[k, :1] += cxd[k, :1] * xlo[sweep, k : k + 1, :]
        target = out_ref if sweep == SWEEPS - 2 else ubuf
        for k in range(LAYERS):
            target[k] = (1.0 - RELAXATION) * ubuf[k] + inv[k] * (part[k] + extra[k])

    for c in halo_copies + sends:
        c.wait_send()
    for d in range(others):
        fault_copy(d).wait_send()
        a_copy(d).wait_send()
        for sweep in range(SWEEPS - 1):
            copy(
                uown.at[sweep, d], urecv.at[sweep, others - 1 - d],
                u_ss.at[sweep, d], u_rs.at[sweep, others - 1 - d], (sector_of(d + 1), t),
            ).wait_send()

    @pl.loop(1, n_slab)
    def _(k):
        b_copy(k, t).wait_send()


def body(n_sector, n_slab, *args):
    vmem = pl.BlockSpec(memory_space=pltpu.VMEM)
    others = n_sector - 1
    rounds = SWEEPS - 1
    block = (LAYERS, ROWS, COLS)
    tiles = (CHUNKS, 128)

    def f32(*shape):
        return pltpu.VMEM(shape, F32)

    def i32(*shape):
        return pltpu.VMEM(shape, jnp.int32)

    def sem(*shape):
        return pltpu.SemaphoreType.DMA(shape)

    scratch = dict(
        p_ref=f32(*block),
        s_ref=f32(2, *block),
        om_ref=f32(3, *block),
        pv_ref=f32(*block),
        tr_ref=f32(3, *block),
        bits_ref=i32(*block),
        fc_ref=i32(1, 1, n_sector, SLOTS),
        cnt_ref=pltpu.SMEM((1, 1, n_sector), jnp.int32),
        ft_ref=f32(1, 1, n_sector, SLOTS),
        fu_ref=i32(1, 1, n_sector, SLOTS),
        in_sem=sem(10),
        oh=pltpu.VMEM((others, CELLS_HI, SLOTS), BF),
        ohlo=pltpu.VMEM((others, 128, SLOTS), BF),
        fsplit=pltpu.VMEM((3, 384, CELLS_HI), BF),
        cell=i32(others, *tiles),
        fweight=f32(others, *tiles),
        fup=i32(others, *tiles),
        own=f32(others, 4, *tiles),
        far=f32(others, 4, *tiles),
        link=f32(others, *tiles),
        vals=f32(others, 4, *tiles),
        up_stage=f32(5, ROWS, COLS),
        dn_stage=f32(3, ROWS, COLS),
        halo_lo=f32(5, ROWS, COLS),
        halo_hi=f32(3, ROWS, COLS),
        rup_stage=f32(5, LAYERS, COLS),
        rdn_stage=f32(3, LAYERS, COLS),
        rhalo_lo=f32(5, LAYERS, COLS),
        rhalo_hi=f32(3, LAYERS, COLS),
        asend=f32(16, 128),
        arecv=f32(others, 16, 128),
        bsend=f32(4, 128),
        brecv=f32(n_slab, 4, 128),
        cz=f32(LAYERS + 1, ROWS, COLS),
        cxu=f32(*block),
        cxd=f32(*block),
        cyu=f32(*block),
        cyd=f32(*block),
        storage=f32(*block),
        rhs=f32(*block),
        inv=f32(*block),
        ubuf=f32(*block),
        part=f32(*block),
        uown=f32(rounds, others, *tiles),
        urecv=f32(rounds, others, *tiles),
        usend=f32(rounds, 2, ROWS, COLS),
        zlo=f32(rounds, ROWS, COLS),
        zhi=f32(rounds, ROWS, COLS),
        xup=f32(rounds, LAYERS, COLS),
        xdn=f32(rounds, LAYERS, COLS),
        xlo=f32(rounds, LAYERS, COLS),
        xhi=f32(rounds, LAYERS, COLS),
        f_ss=sem(others), f_rs=sem(others),
        h_ss=sem(4), h_rs=sem(4),
        a_ss=sem(others), a_rs=sem(others),
        b_ss=sem(n_slab - 1), b_rs=sem(n_slab - 1),
        u_ss=sem(rounds, others), u_rs=sem(rounds, others),
        w_ss=sem(rounds, 4), w_rs=sem(rounds, 4),
    )
    names = list(scratch)

    def run(*refs):
        kernel(n_sector, n_slab, refs[:10], *refs[10:12], **dict(zip(names, refs[12:])))

    return pl.pallas_call(
        run,
        out_shape=(
            jax.ShapeDtypeStruct((3, *block), F32),
            jax.ShapeDtypeStruct(block, F32),
        ),
        in_specs=[pl.BlockSpec(memory_space=pltpu.HBM)] * 10,
        out_specs=(vmem, vmem),
        scratch_shapes=list(scratch.values()),
        compiler_params=pltpu.CompilerParams(
            collective_id=0, has_side_effects=True, vmem_limit_bytes=60 * 2**20
        ),
    )(*args)


def solution(mesh):
    placed = (
        P("slab", "sector", None),
        P(None, "slab", "sector", None),
        P(None, "slab", "sector", None),
        P("slab", "sector", None),
        P(None, "slab", "sector", None),
        P("slab", "sector", None),
        P("slab", "sector", None, None),
        P("slab", "sector", None),
        P("slab", "sector", None, None),
        P("slab", "sector", None, None),
    )
    return jax.shard_map(
        functools.partial(body, mesh.shape["sector"], mesh.shape["slab"]),
        mesh=mesh,
        in_specs=placed,
        out_specs=(P(None, "slab", "sector", None), P("slab", "sector", None)),
        check_vma=False,
    )
```

```python
import functools

import jax
import jax.numpy as jnp
from jax import lax
from jax.experimental import pallas as pl
from jax.experimental.pallas import tpu as pltpu
from jax.sharding import PartitionSpec as P

COMPRESS = (0.0002, 0.0005, 0.002)
VISCOSITY = (1.0, 3.0, 0.5)
RELAXATION = 2.0 / 3.0
SWEEPS = 4

BF = jnp.bfloat16
F32 = jnp.float32
MESH = pl.DeviceIdType.MESH

LAYERS, ROWS, COLS = 4, 64, 128
CELLS_HI = LAYERS * ROWS
SLOTS = 1024
CHUNKS = SLOTS // 128


def split(value, count):
    parts = []
    for _ in range(count - 1):
        part = value.astype(BF)
        parts.append(part)
        value = value - part.astype(F32)
    parts.append(value.astype(BF))
    return parts


def mobilities(s_water, s_gas):
    s_oil = 1.0 - s_water - s_gas
    return [s * s * (1.0 / v) for s, v in zip((s_water, s_oil, s_gas), VISCOSITY)]


def face(p_low, m_low, weight, words, p_high, m_high, first_bit):
    drop = p_low - p_high
    fluxes, total = [], None
    for a in range(3):
        flag = jnp.bitwise_and(words, 1 << (first_bit + a)) != 0
        part = weight * jnp.where(flag, m_low[a], m_high[a])
        fluxes.append(part * drop)
        total = part if total is None else total + part
    return fluxes, total


def kernel(
    n_sector, n_slab,
    inputs, res_ref, out_ref, *,
    p_ref, s_ref, om_ref, pv_ref, tr_ref, bits_ref, fc_ref, cnt_ref, ft_ref, fu_ref, in_sem,
    oh, ohlo, fsplit, cell, fweight, fup, own, far, link, vals,
    up_stage, dn_stage, halo_lo, halo_hi, rup_stage, rdn_stage, rhalo_lo, rhalo_hi,
    asend, arecv, bsend, brecv,
    cz, cxu, cxd, cyu, cyd, storage, rhs, inv, ubufs, part, to_layer,
    uown, urecv, zlo, zhi, xup, xdn, xlo, xhi,
    f_ss, f_rs, h_ss, h_rs, a_ss, a_rs, b_ss, b_rs, u_ss, u_rs, w_ss, w_rs,
):
    me = lax.axis_index("sector")
    t = lax.axis_index("slab")
    others = n_sector - 1
    s_next = lax.rem(me + 1, n_sector)
    s_prev = lax.rem(me + n_sector - 1, n_sector)
    t_next = lax.rem(t + 1, n_slab)
    t_prev = lax.rem(t + n_slab - 1, n_slab)

    def copy(src, dst, ss, rs, device):
        return pltpu.make_async_remote_copy(
            src_ref=src, dst_ref=dst, send_sem=ss, recv_sem=rs,
            device_id=device, device_id_type=MESH,
        )

    chips = n_sector // 2
    reach = sorted(range(1, chips), key=lambda c: (-min(c, chips - c), c))
    partners = [(c, other) for c in reach for other in (0, 1)] + [(0, 1)]
    mirror = [partners.index(((chips - c) % chips, other)) for c, other in partners]
    chip, core = me // 2, lax.rem(me, 2)

    def sector_of(i):
        c, other = partners[i]
        return lax.rem(chip + c, chips) * 2 + (1 - core if other else core)

    held = (p_ref, s_ref, om_ref, pv_ref, tr_ref, bits_ref, fc_ref, cnt_ref, ft_ref, fu_ref)
    loads = [
        pltpu.make_async_copy(src, dst, in_sem.at[i])
        for i, (src, dst) in enumerate(zip(inputs, held))
    ]
    for i in (6, 7, 8, 9, 0, 1, 4, 5, 3, 2):
        loads[i].start()
    barrier = pltpu.get_barrier_semaphore()

    for i in range(others):
        pl.semaphore_signal(barrier, inc=1, device_id=(sector_of(i), t), device_id_type=MESH)

    @pl.loop(1, n_slab)
    def _(k):
        pl.semaphore_signal(
            barrier, inc=1, device_id=(me, lax.rem(t + k, n_slab)), device_id_type=MESH
        )

    for i in (6, 7, 8, 9, 0, 1, 4, 5):
        loads[i].wait()
    top = LAYERS - 1
    for i, plane in enumerate((p_ref[0], s_ref[0, 0], s_ref[1, 0])):
        dn_stage[i] = plane
    last = ROWS - 1
    for k in range(LAYERS):
        for i, row in enumerate(
            (p_ref[k, last:], s_ref[0, k, last:], s_ref[1, k, last:], tr_ref[1, k, last:])
        ):
            rup_stage[i, k : k + 1, :] = row
        rup_stage[4, k : k + 1, :] = bits_ref[k, last:].astype(F32)
        for i, row in enumerate((p_ref[k, :1], s_ref[0, k, :1], s_ref[1, k, :1])):
            rdn_stage[i, k : k + 1, :] = row

    lane = lax.broadcasted_iota(jnp.int32, (1, 128), 1)
    counts = [cnt_ref[0, 0, sector_of(d)] for d in range(others)]
    turn = lax.rem(n_sector - 2 * chip, n_sector)
    first_core = core == 0
    for b in range(CHUNKS):
        span = slice(b * 128, (b + 1) * 128)
        cells = pltpu.roll(fc_ref[0, 0, :, span], turn, 0)
        flags = pltpu.roll(fu_ref[0, 0, :, span], turn, 0)
        trans = pltpu.roll(ft_ref[0, 0, :, span], turn, 0)
        for d, (c, other) in enumerate(partners):
            here, there = 2 * c + other, 2 * c + 1 - other

            def pick(x):
                return jnp.where(first_core, x[here : here + 1], x[there : there + 1])

            cell[d, b : b + 1, :] = pick(cells)
            fup[d, b : b + 1, :] = pick(flags)
            fweight[d, b : b + 1, :] = jnp.where(lane + b * 128 < counts[d], pick(trans), 0.0)

    for i, field in enumerate((p_ref, s_ref.at[0], s_ref.at[1])):
        flipped = field[...].reshape(CELLS_HI, COLS).T
        for j, piece in enumerate(split(flipped, 3)):
            fsplit[i, j * 128 : (j + 1) * 128, :] = piece

    sub = lax.broadcasted_iota(jnp.int32, (128, 128), 0)
    sub_hi = lax.broadcasted_iota(jnp.int32, (CELLS_HI, 128), 0)

    @pl.loop(0, others)
    def _(d):
        for b in range(CHUNKS):
            span = slice(b * 128, (b + 1) * 128)
            c = cell[d, b : b + 1, :]
            oh[d, :, span] = jnp.where(sub_hi == jnp.right_shift(c, 7), 1.0, 0.0).astype(BF)
            ohlo[d, :, span] = jnp.where(sub == jnp.bitwise_and(c, 127), 1.0, 0.0).astype(BF)

    def gather(d, weights, count, store):
        rows = [jnp.bitwise_and(cell[d, b : b + 1, :], 127) for b in range(CHUNKS)]
        for i, w in enumerate(weights):
            for b in range(CHUNKS // 2):
                picks = oh[d, :, b * 256 : (b + 1) * 256]
                g = jnp.dot(w, picks, preferred_element_type=F32)
                total = g[(count - 1) * 128 :]
                for j in reversed(range(count - 1)):
                    total = g[j * 128 : (j + 1) * 128] + total
                for k in range(2):
                    found = jnp.where(
                        sub == rows[2 * b + k], total[:, k * 128 : (k + 1) * 128], 0.0
                    )
                    store(i, 2 * b + k, jnp.sum(found, axis=0, keepdims=True))

    def fault_copy(d):
        return copy(own.at[d], far.at[mirror[d]], f_ss.at[d], f_rs.at[mirror[d]],
                    (sector_of(d), t))

    for d in range(others):

        def store(i, b, row, d=d):
            own[d, i, b : b + 1, :] = row

        gather(d, [fsplit[i] for i in range(3)], 3, store)
        own[d, 3] = jnp.right_shift(cell[d], 13).astype(F32)

    lane2 = lax.broadcasted_iota(jnp.int32, (ROWS, COLS), 1)
    row2 = lax.broadcasted_iota(jnp.int32, (ROWS, COLS), 0)
    not_first_slab = jnp.where(t > 0, 1.0, 0.0).astype(F32)
    not_last_slab = jnp.where(t < n_slab - 1, 1.0, 0.0).astype(F32)
    not_first_sector = jnp.where(me > 0, 1.0, 0.0).astype(F32)
    not_last_sector = jnp.where(me < n_sector - 1, 1.0, 0.0).astype(F32)

    loads[3].wait()
    loads[2].wait()
    for k in range(LAYERS):
        p = p_ref[k]
        pv = pv_ref[k]
        sw, sg = s_ref[0, k], s_ref[1, k]
        so = 1.0 - sw - sg
        m = mobilities(sw, sg)
        words = bits_ref[k]
        sat = (sw, so, sg)
        st = pv * (sw * COMPRESS[0] + so * COMPRESS[1] + sg * COMPRESS[2])
        storage[k] = st
        res = [pv * sat[a] * (1.0 + COMPRESS[a] * p) - om_ref[a, k] for a in range(3)]
        flux, coupling = face(
            p, m, jnp.where(lane2 < COLS - 1, tr_ref[2, k], 0.0), words,
            pltpu.roll(p, COLS - 1, 1), [pltpu.roll(x, COLS - 1, 1) for x in m], 6,
        )
        res = [res[a] + (flux[a] - pltpu.roll(flux[a], 1, 1)) for a in range(3)]
        back = pltpu.roll(coupling, 1, 1)
        cyu[k] = coupling
        cyd[k] = back
        inv[k] = st + (coupling + back)
        for a in range(3):
            res_ref[a, k] = res[a]
        if k > 0:
            flux, coupling = face(
                p_ref[k - 1], mobilities(s_ref[0, k - 1], s_ref[1, k - 1]), tr_ref[0, k - 1],
                bits_ref[k - 1], p, m, 0,
            )
            cz[k] = coupling
            inv[k] += coupling
            inv[k - 1] += coupling
            for a in range(3):
                res_ref[a, k] -= flux[a]
                res_ref[a, k - 1] += flux[a]

    pl.semaphore_wait(barrier, n_sector - 1 + n_slab - 1)

    halo_copies = [
        copy(dn_stage, halo_hi, h_ss.at[1], h_rs.at[1], (me, t_prev)),
        copy(rup_stage, rhalo_lo, h_ss.at[2], h_rs.at[2], (s_next, t)),
        copy(rdn_stage, rhalo_hi, h_ss.at[3], h_rs.at[3], (s_prev, t)),
    ]
    for c in halo_copies:
        c.start()
    for d in range(others):
        fault_copy(d).start()

    zero_tile = jnp.zeros((CHUNKS, 128), F32)
    layer_source = [zero_tile] * LAYERS
    for d in range(others):
        fault_copy(d).wait_recv()
    for d in range(others):
        flags = fup[d]
        w = fweight[d]
        flux, coupling = face(
            own[d, 0], mobilities(own[d, 1], own[d, 2]), w, flags,
            far[d, 0], mobilities(far[d, 1], far[d, 2]), 0,
        )
        for a in range(3):
            vals[d, a] = flux[a]
        vals[d, 3] = coupling
        link[d] = coupling
        layer = jnp.right_shift(cell[d], 13)
        for k in range(LAYERS):
            layer_source[k] = layer_source[k] - jnp.where(layer == k, flux[2], 0.0)

    nt = (((1,), (1,)), ((), ()))

    def masked(d, field):
        pieces = []
        for b in range(CHUNKS):
            mask = ohlo[d, :, b * 128 : (b + 1) * 128]
            parts = split(field[b : b + 1, :], 2)
            pieces.append(jnp.concatenate([mask * x for x in parts], 0))
        return jnp.concatenate(pieces, 1)

    def scatter(fields):
        total = None
        for d in range(others):
            rows = jnp.concatenate([masked(d, vals.at[d, i]) for i in fields], 0)
            part = lax.dot_general(rows, oh[d], nt, preferred_element_type=F32)
            total = part if total is None else total + part
        return [
            (total[256 * i : 256 * i + 128] + total[256 * i + 128 : 256 * i + 256])
            .T.reshape(LAYERS, ROWS, COLS)
            for i in range(len(fields))
        ]

    placed = scatter((0, 1))
    res_ref[0] += placed[0]
    res_ref[1] += placed[1]

    for c in halo_copies:
        c.wait_recv()

    p = p_ref[top]
    m = mobilities(s_ref[0, top], s_ref[1, top])
    flux, coupling = face(
        p, m, tr_ref[0, top] * not_last_slab, bits_ref[top],
        halo_hi[0], mobilities(halo_hi[1], halo_hi[2]), 0,
    )
    cz[LAYERS] = coupling
    inv[top] += coupling
    for a in range(3):
        res_ref[a, top] += flux[a]
        up_stage[a] = flux[a]
    up_stage[3] = coupling
    asend[12:13, :] = jnp.sum(flux[0] + flux[1] + flux[2], axis=0, keepdims=True)
    asend[13:16, :] = jnp.zeros((3, 128), F32)
    up_copy = copy(up_stage, halo_lo, h_ss.at[0], h_rs.at[0], (me, t_next))

    first_p = rdn_stage[0]
    low_flux, low_link = face(
        rhalo_lo[0], mobilities(rhalo_lo[1], rhalo_lo[2]), rhalo_lo[3] * not_first_sector,
        rhalo_lo[4].astype(jnp.int32), first_p, mobilities(rdn_stage[1], rdn_stage[2]), 3,
    )
    hi_m = mobilities(rhalo_hi[1], rhalo_hi[2])
    for k in range(LAYERS):
        p = p_ref[k]
        m = mobilities(s_ref[0, k], s_ref[1, k])

        def after(x, edge):
            return jnp.where(row2 == last, edge[k : k + 1], pltpu.roll(x, last, 0))

        def before(x, edge):
            return jnp.where(row2 == 0, edge[k : k + 1], pltpu.roll(x, 1, 0))

        weight = tr_ref[1, k] * jnp.where(row2 == last, not_last_sector, 1.0)
        flux, coupling = face(
            p, m, weight, bits_ref[k], after(p, rhalo_hi[0]),
            [after(m[a], hi_m[a]) for a in range(3)], 3,
        )
        back = before(coupling, low_link)
        cxu[k] = coupling
        cxd[k] = back
        inv[k] += coupling + back
        for a in range(3):
            res_ref[a, k] += flux[a] - before(flux[a], low_flux[a])

    for k in range(LAYERS):
        regular = -(res_ref[0, k] + res_ref[1, k] + res_ref[2, k])
        source = jnp.sum(regular, axis=0, keepdims=True) + jnp.sum(
            layer_source[k], axis=0, keepdims=True
        )
        asend[k : k + 1, :] = jnp.sum(storage[k], axis=0, keepdims=True)
        asend[4 + k : 5 + k, :] = jnp.sum(cz[k + 1], axis=0, keepdims=True)
        asend[8 + k : 9 + k, :] = source

    def a_copy(d):
        return copy(asend, arecv.at[mirror[d]], a_ss.at[d], a_rs.at[mirror[d]],
                    (sector_of(d), t))

    for d in range(others):
        a_copy(d).start()
    up_copy.start()

    placed = scatter((2, 3))
    res_ref[2] += placed[0]
    inv[...] += placed[1]

    sums = asend[...]
    for d in range(others):
        a_copy(d).wait_recv()
    for d in range(others):
        sums = sums + arecv[d]
    column = jnp.sum(sums, axis=1, keepdims=True)
    lane16 = lax.broadcasted_iota(jnp.int32, (16, 128), 1)
    row16 = lax.broadcasted_iota(jnp.int32, (16, 128), 0)
    spread = jnp.where(
        jnp.bitwise_and(lane16, 3) == jnp.bitwise_and(row16, 3),
        jnp.broadcast_to(column, (16, 128)), 0.0,
    )
    for q in range(4):
        bsend[q : q + 1, :] = jnp.sum(spread[4 * q : 4 * q + 4], axis=0, keepdims=True)
    brecv[t] = bsend[...]

    def b_copy(k, dst):
        return copy(bsend, brecv.at[dst], b_ss.at[k - 1], b_rs.at[k - 1],
                    (me, lax.rem(t + k, n_slab)))

    def hops(k):
        z, y, across = k % 8, k // 8, n_slab // 8
        return min(z, 8 - z) + min(y, across - y)

    for k in sorted(range(1, n_slab), key=lambda k: (-hops(k), k)):
        b_copy(k, t).start()

    for d in range(others):
        for j in range(LAYERS):
            vals[d, j] = jnp.where(far[d, 3] == j, link[d], 0.0)
    for j in range(0, LAYERS, 2):
        placed = scatter((j, j + 1))
        to_layer[j] = placed[0]
        to_layer[j + 1] = placed[1]

    up_copy.wait_recv()
    cz[0] = halo_lo[3]
    inv[0] += halo_lo[3]
    for a in range(3):
        res_ref[a, 0] -= halo_lo[a]
    inv[...] = RELAXATION / inv[...]
    for k in range(LAYERS):
        rhs[k] = -(res_ref[0, k] + res_ref[1, k] + res_ref[2, k])

    @pl.loop(1, n_slab)
    def _(k):
        b_copy(k, lax.rem(t + n_slab - k, n_slab)).wait_recv()

    lane4 = lax.broadcasted_iota(jnp.int32, (4, 128), 1)
    rows = jnp.zeros((4, 128), F32)
    for j in range(n_slab):
        rows = rows + jnp.where(jnp.right_shift(lane4, 2) == j, brecv[j], 0.0)
    s_row, right = rows[0:1], rows[1:2]
    rhs_row = rows[2:3] + pltpu.roll(rows[3:4], LAYERS, 1)
    lane1 = lax.broadcasted_iota(jnp.int32, (1, 128), 1)
    right = jnp.where(lane1 < LAYERS * n_slab - 1, right, 0.0)
    s_row = jnp.where(lane1 < LAYERS * n_slab, s_row, 1.0)
    left = jnp.where(lane1 > 0, pltpu.roll(right, 1, 1), 0.0)
    step = 1
    while step < LAYERS * n_slab:
        pivot = 1.0 / (s_row + left + right)
        sn, ln, rn, dn = s_row * pivot, left * pivot, right * pivot, rhs_row * pivot
        s_row = s_row + left * pltpu.roll(sn, step, 1) + right * pltpu.roll(sn, 128 - step, 1)
        rhs_row = rhs_row + left * pltpu.roll(dn, step, 1) + right * pltpu.roll(dn, 128 - step, 1)
        left = left * pltpu.roll(ln, step, 1)
        right = right * pltpu.roll(rn, 128 - step, 1)
        step *= 2
    coarse = rhs_row / s_row
    lane8 = lax.broadcasted_iota(jnp.int32, (8, 128), 1)
    row8 = lax.broadcasted_iota(jnp.int32, (8, 128), 0)
    level = jnp.sum(
        jnp.where(lane8 == row8 + (LAYERS * t - 1), jnp.broadcast_to(coarse, (8, 128)), 0.0),
        axis=1, keepdims=True,
    )
    level = jnp.broadcast_to(level, (8, 128))

    def level_row(k):
        return level[k + 1 : k + 2]

    for k in range(LAYERS):
        here = level_row(k)
        total = rhs[k] + cz[k + 1] * level_row(k + 1) + cz[k] * level_row(k - 1)
        total = total + (cxu[k] + cxd[k] + cyu[k] + cyd[k]) * here
        for j in range(LAYERS):
            total = total + to_layer[j, k] * level_row(j)
        ubufs[0, k] = (1.0 - RELAXATION) * here + inv[k] * total

    block_shape = (LAYERS, ROWS, COLS)
    groups = [list(range(2)), list(range(2, 4)), list(range(4, others))]
    sends = []
    for sweep in range(SWEEPS - 1):
        ubuf = ubufs.at[sweep]
        edge_copies = [
            copy(ubufs.at[sweep, top], zlo.at[sweep], w_ss.at[sweep, 0], w_rs.at[sweep, 0], (me, t_next)),
            copy(ubufs.at[sweep, 0], zhi.at[sweep], w_ss.at[sweep, 1], w_rs.at[sweep, 1], (me, t_prev)),
            copy(xup.at[sweep], xlo.at[sweep], w_ss.at[sweep, 2], w_rs.at[sweep, 2], (s_next, t)),
            copy(xdn.at[sweep], xhi.at[sweep], w_ss.at[sweep, 3], w_rs.at[sweep, 3], (s_prev, t)),
        ]
        edge_copies[0].start()
        edge_copies[1].start()
        sends += edge_copies
        flipped = ubuf[...].reshape(CELLS_HI, COLS).T
        weights = jnp.concatenate(split(flipped, 2), 0)
        fsplit[0, :256, :] = weights

        def u_copy(d, sweep=sweep):
            return copy(
                uown.at[sweep, d], urecv.at[sweep, mirror[d]],
                u_ss.at[sweep, d], u_rs.at[sweep, mirror[d]], (sector_of(d), t),
            )

        weights = fsplit[0, :256]
        for group in groups:
            for d in group:

                def store(i, b, row, d=d):
                    uown[sweep, d, b : b + 1, :] = row

                gather(d, [weights], 2, store)
            if group is groups[1]:
                for k in range(LAYERS):
                    xup[sweep, k : k + 1, :] = ubuf[k, last:]
                    xdn[sweep, k : k + 1, :] = ubuf[k, :1]
            for d in group:
                u_copy(d).start()
            if group is groups[1]:
                edge_copies[2].start()
                edge_copies[3].start()

        for k in range(LAYERS):
            u = ubuf[k]
            total = rhs[k] + cyu[k] * pltpu.roll(u, COLS - 1, 1) + cyd[k] * pltpu.roll(u, 1, 1)
            total = total + cxu[k] * jnp.where(row2 == last, 0.0, pltpu.roll(u, last, 0))
            total = total + cxd[k] * jnp.where(row2 == 0, 0.0, pltpu.roll(u, 1, 0))
            if k > 0:
                total = total + cz[k] * ubuf[k - 1]
            if k < top:
                total = total + cz[k + 1] * ubuf[k + 1]
            part[k] = total

        total = None
        for group in (groups[0] + groups[1], groups[2]):
            for i in group:
                u_copy(i).wait_recv()
            for d in [mirror[i] for i in group]:
                vals[d, 0] = link[d] * urecv[sweep, d]
                placed = lax.dot_general(
                    oh[d], masked(d, vals.at[d, 0]), nt, preferred_element_type=F32
                )
                total = placed if total is None else total + placed
        extra = (total[:, :128] + total[:, 128:]).reshape(block_shape)
        for c in edge_copies:
            c.wait_recv()
        part[0] += cz[0] * zlo[sweep]
        part[top] += cz[LAYERS] * zhi[sweep]
        for k in range(LAYERS):
            part[k, last:] += cxu[k, last:] * xhi[sweep, k : k + 1, :]
            part[k, :1] += cxd[k, :1] * xlo[sweep, k : k + 1, :]
        target = out_ref if sweep == SWEEPS - 2 else ubufs.at[sweep + 1]
        for k in range(LAYERS):
            target[k] = (1.0 - RELAXATION) * ubuf[k] + inv[k] * (part[k] + extra[k])

    for c in halo_copies + [up_copy] + sends:
        c.wait_send()
    for d in range(others):
        fault_copy(d).wait_send()
        a_copy(d).wait_send()
        for sweep in range(SWEEPS - 1):
            copy(
                uown.at[sweep, d], urecv.at[sweep, mirror[d]],
                u_ss.at[sweep, d], u_rs.at[sweep, mirror[d]], (sector_of(d), t),
            ).wait_send()

    @pl.loop(1, n_slab)
    def _(k):
        b_copy(k, t).wait_send()


def body(n_sector, n_slab, *args):
    vmem = pl.BlockSpec(memory_space=pltpu.VMEM)
    others = n_sector - 1
    rounds = SWEEPS - 1
    block = (LAYERS, ROWS, COLS)
    tiles = (CHUNKS, 128)

    def f32(*shape):
        return pltpu.VMEM(shape, F32)

    def i32(*shape):
        return pltpu.VMEM(shape, jnp.int32)

    def sem(*shape):
        return pltpu.SemaphoreType.DMA(shape)

    scratch = dict(
        p_ref=f32(*block),
        s_ref=f32(2, *block),
        om_ref=f32(3, *block),
        pv_ref=f32(*block),
        tr_ref=f32(3, *block),
        bits_ref=i32(*block),
        fc_ref=i32(1, 1, n_sector, SLOTS),
        cnt_ref=pltpu.SMEM((1, 1, n_sector), jnp.int32),
        ft_ref=f32(1, 1, n_sector, SLOTS),
        fu_ref=i32(1, 1, n_sector, SLOTS),
        in_sem=sem(10),
        oh=pltpu.VMEM((others, CELLS_HI, SLOTS), BF),
        ohlo=pltpu.VMEM((others, 128, SLOTS), BF),
        fsplit=pltpu.VMEM((3, 384, CELLS_HI), BF),
        cell=i32(others, *tiles),
        fweight=f32(others, *tiles),
        fup=i32(others, *tiles),
        own=f32(others, 4, *tiles),
        far=f32(others, 4, *tiles),
        link=f32(others, *tiles),
        vals=f32(others, 4, *tiles),
        up_stage=f32(4, ROWS, COLS),
        dn_stage=f32(3, ROWS, COLS),
        halo_lo=f32(4, ROWS, COLS),
        halo_hi=f32(3, ROWS, COLS),
        rup_stage=f32(5, LAYERS, COLS),
        rdn_stage=f32(3, LAYERS, COLS),
        rhalo_lo=f32(5, LAYERS, COLS),
        rhalo_hi=f32(3, LAYERS, COLS),
        asend=f32(16, 128),
        arecv=f32(others, 16, 128),
        bsend=f32(4, 128),
        brecv=f32(n_slab, 4, 128),
        cz=f32(LAYERS + 1, ROWS, COLS),
        cxu=f32(*block),
        cxd=f32(*block),
        cyu=f32(*block),
        cyd=f32(*block),
        storage=f32(*block),
        rhs=f32(*block),
        inv=f32(*block),
        ubufs=f32(rounds, *block),
        part=f32(*block),
        to_layer=f32(LAYERS, *block),
        uown=f32(rounds, others, *tiles),
        urecv=f32(rounds, others, *tiles),
        zlo=f32(rounds, ROWS, COLS),
        zhi=f32(rounds, ROWS, COLS),
        xup=f32(rounds, LAYERS, COLS),
        xdn=f32(rounds, LAYERS, COLS),
        xlo=f32(rounds, LAYERS, COLS),
        xhi=f32(rounds, LAYERS, COLS),
        f_ss=sem(others), f_rs=sem(others),
        h_ss=sem(4), h_rs=sem(4),
        a_ss=sem(others), a_rs=sem(others),
        b_ss=sem(n_slab - 1), b_rs=sem(n_slab - 1),
        u_ss=sem(rounds, others), u_rs=sem(rounds, others),
        w_ss=sem(rounds, 4), w_rs=sem(rounds, 4),
    )
    names = list(scratch)

    def run(*refs):
        kernel(n_sector, n_slab, refs[:10], *refs[10:12], **dict(zip(names, refs[12:])))

    return pl.pallas_call(
        run,
        out_shape=(
            jax.ShapeDtypeStruct((3, *block), F32),
            jax.ShapeDtypeStruct(block, F32),
        ),
        in_specs=[pl.BlockSpec(memory_space=pltpu.HBM)] * 10,
        out_specs=(vmem, vmem),
        scratch_shapes=list(scratch.values()),
        compiler_params=pltpu.CompilerParams(
            collective_id=0, has_side_effects=True, vmem_limit_bytes=60 * 2**20
        ),
    )(*args)


def solution(mesh):
    placed = (
        P("slab", "sector", None),
        P(None, "slab", "sector", None),
        P(None, "slab", "sector", None),
        P("slab", "sector", None),
        P(None, "slab", "sector", None),
        P("slab", "sector", None),
        P("slab", "sector", None, None),
        P("slab", "sector", None),
        P("slab", "sector", None, None),
        P("slab", "sector", None, None),
    )
    return jax.shard_map(
        functools.partial(body, mesh.shape["sector"], mesh.shape["slab"]),
        mesh=mesh,
        in_specs=placed,
        out_specs=(P(None, "slab", "sector", None), P("slab", "sector", None)),
        check_vma=False,
    )
```

```python
import functools

import jax
import jax.numpy as jnp
from jax import lax
from jax.experimental import pallas as pl
from jax.experimental.pallas import tpu as pltpu
from jax.sharding import PartitionSpec as P

COMPRESS = (0.0002, 0.0005, 0.002)
VISCOSITY = (1.0, 3.0, 0.5)
RELAXATION = 2.0 / 3.0
SWEEPS = 4

BF = jnp.bfloat16
F32 = jnp.float32
MESH = pl.DeviceIdType.MESH

LAYERS, ROWS, COLS = 4, 64, 128
CELLS_HI = LAYERS * ROWS
SLOTS = 1024
CHUNKS = SLOTS // 128


def split(value, count):
    parts = []
    for _ in range(count - 1):
        part = value.astype(BF)
        parts.append(part)
        value = value - part.astype(F32)
    parts.append(value.astype(BF))
    return parts


def mobilities(s_water, s_gas):
    s_oil = 1.0 - s_water - s_gas
    return [s * s * (1.0 / v) for s, v in zip((s_water, s_oil, s_gas), VISCOSITY)]


def face(p_low, m_low, weight, words, p_high, m_high, first_bit):
    drop = p_low - p_high
    fluxes, total = [], None
    for a in range(3):
        flag = jnp.bitwise_and(words, 1 << (first_bit + a)) != 0
        part = weight * jnp.where(flag, m_low[a], m_high[a])
        fluxes.append(part * drop)
        total = part if total is None else total + part
    return fluxes, total


def kernel(
    n_sector, n_slab,
    inputs, res_ref, out_ref, *,
    p_ref, s_ref, om_ref, pv_ref, tr_ref, bits_ref, fc_ref, cnt_ref, ft_ref, fu_ref, in_sem,
    oh, ohlo, fsplit, cell, fweight, fup, own, far, link, vals,
    up_stage, dn_stage, halo_lo, halo_hi, rup_stage, rdn_stage, rhalo_lo, rhalo_hi,
    asend, arecv, bsend, brecv,
    cz, cxu, cxd, cyu, cyd, storage, rhs, inv, ubufs, part,
    uown, urecv, zlo, zhi, xup, xdn, xlo, xhi,
    f_ss, f_rs, h_ss, h_rs, a_ss, a_rs, b_ss, b_rs, u_ss, u_rs, w_ss, w_rs,
):
    me = lax.axis_index("sector")
    t = lax.axis_index("slab")
    others = n_sector - 1
    s_next = lax.rem(me + 1, n_sector)
    s_prev = lax.rem(me + n_sector - 1, n_sector)
    t_next = lax.rem(t + 1, n_slab)
    t_prev = lax.rem(t + n_slab - 1, n_slab)

    def copy(src, dst, ss, rs, device):
        return pltpu.make_async_remote_copy(
            src_ref=src, dst_ref=dst, send_sem=ss, recv_sem=rs,
            device_id=device, device_id_type=MESH,
        )

    chips = n_sector // 2
    reach = sorted(range(1, chips), key=lambda c: (-min(c, chips - c), c))
    partners = [(c, other) for c in reach for other in (0, 1)] + [(0, 1)]
    mirror = [partners.index(((chips - c) % chips, other)) for c, other in partners]
    chip, core = me // 2, lax.rem(me, 2)

    sectors = [
        lax.rem(chip + c, chips) * 2 + (1 - core if other else core) for c, other in partners
    ]

    def sector_of(i):
        return sectors[i]

    def take(ref, sem):
        copy(ref, ref, sem, sem, (s_next, t)).wait_recv()

    def sent(ref, sem):
        copy(ref, ref, sem, sem, (s_next, t)).wait_send()

    held = (p_ref, s_ref, om_ref, pv_ref, tr_ref, bits_ref, fc_ref, cnt_ref, ft_ref, fu_ref)
    loads = [
        pltpu.make_async_copy(src, dst, in_sem.at[i])
        for i, (src, dst) in enumerate(zip(inputs, held))
    ]
    for i in (6, 7, 8, 9, 0, 1, 4, 5, 3, 2):
        loads[i].start()
    barrier = pltpu.get_barrier_semaphore()

    for i in range(others):
        pl.semaphore_signal(barrier, inc=1, device_id=(sector_of(i), t), device_id_type=MESH)

    @pl.loop(1, n_slab)
    def _(k):
        pl.semaphore_signal(
            barrier, inc=1, device_id=(me, lax.rem(t + k, n_slab)), device_id_type=MESH
        )

    for i in (6, 7, 8, 9, 0, 1, 4, 5):
        loads[i].wait()
    top = LAYERS - 1
    for i, plane in enumerate((p_ref[0], s_ref[0, 0], s_ref[1, 0])):
        dn_stage[i] = plane
    last = ROWS - 1
    for k in range(LAYERS):
        for i, row in enumerate(
            (p_ref[k, last:], s_ref[0, k, last:], s_ref[1, k, last:], tr_ref[1, k, last:])
        ):
            rup_stage[i, k : k + 1, :] = row
        rup_stage[4, k : k + 1, :] = bits_ref[k, last:].astype(F32)
        for i, row in enumerate((p_ref[k, :1], s_ref[0, k, :1], s_ref[1, k, :1])):
            rdn_stage[i, k : k + 1, :] = row

    lane = lax.broadcasted_iota(jnp.int32, (1, 128), 1)
    counts = [cnt_ref[0, 0, sector_of(d)] for d in range(others)]
    turn = lax.rem(n_sector - 2 * chip, n_sector)
    first_core = core == 0
    for b in range(CHUNKS):
        span = slice(b * 128, (b + 1) * 128)
        cells = pltpu.roll(fc_ref[0, 0, :, span], turn, 0)
        flags = pltpu.roll(fu_ref[0, 0, :, span], turn, 0)
        trans = pltpu.roll(ft_ref[0, 0, :, span], turn, 0)
        for d, (c, other) in enumerate(partners):
            here, there = 2 * c + other, 2 * c + 1 - other

            def pick(x):
                return jnp.where(first_core, x[here : here + 1], x[there : there + 1])

            cell[d, b : b + 1, :] = pick(cells)
            fup[d, b : b + 1, :] = pick(flags)
            fweight[d, b : b + 1, :] = jnp.where(lane + b * 128 < counts[d], pick(trans), 0.0)

    for i, field in enumerate((p_ref, s_ref.at[0], s_ref.at[1])):
        flipped = field[...].reshape(CELLS_HI, COLS).T
        for j, piece in enumerate(split(flipped, 3)):
            fsplit[i, j * 128 : (j + 1) * 128, :] = piece

    sub = lax.broadcasted_iota(jnp.int32, (128, 128), 0)
    sub_hi = lax.broadcasted_iota(jnp.int32, (CELLS_HI, 128), 0)

    @pl.loop(0, others)
    def _(d):
        for b in range(CHUNKS):
            span = slice(b * 128, (b + 1) * 128)
            c = cell[d, b : b + 1, :]
            oh[d, :, span] = jnp.where(sub_hi == jnp.right_shift(c, 7), 1.0, 0.0).astype(BF)
            ohlo[d, :, span] = jnp.where(sub == jnp.bitwise_and(c, 127), 1.0, 0.0).astype(BF)

    def gather(d, weights, count, store):
        rows = [jnp.bitwise_and(cell[d, b : b + 1, :], 127) for b in range(CHUNKS)]
        for i, w in enumerate(weights):
            for b in range(CHUNKS // 2):
                picks = oh[d, :, b * 256 : (b + 1) * 256]
                g = jnp.dot(w, picks, preferred_element_type=F32)
                total = g[(count - 1) * 128 :]
                for j in reversed(range(count - 1)):
                    total = g[j * 128 : (j + 1) * 128] + total
                for k in range(2):
                    found = jnp.where(
                        sub == rows[2 * b + k], total[:, k * 128 : (k + 1) * 128], 0.0
                    )
                    store(i, 2 * b + k, jnp.sum(found, axis=0, keepdims=True))

    def fault_copy(d):
        return copy(own.at[d], far.at[mirror[d]], f_ss.at[0], f_rs.at[0],
                    (sector_of(d), t))

    for d in range(others):

        def store(i, b, row, d=d):
            own[d, i, b : b + 1, :] = row

        gather(d, [fsplit[i] for i in range(3)], 3, store)
        own[d, 3] = jnp.right_shift(cell[d], 13).astype(F32)

    lane2 = lax.broadcasted_iota(jnp.int32, (ROWS, COLS), 1)
    row2 = lax.broadcasted_iota(jnp.int32, (ROWS, COLS), 0)
    not_first_slab = jnp.where(t > 0, 1.0, 0.0).astype(F32)
    not_last_slab = jnp.where(t < n_slab - 1, 1.0, 0.0).astype(F32)
    not_first_sector = jnp.where(me > 0, 1.0, 0.0).astype(F32)
    not_last_sector = jnp.where(me < n_sector - 1, 1.0, 0.0).astype(F32)

    loads[3].wait()
    loads[2].wait()
    for k in range(LAYERS):
        p = p_ref[k]
        pv = pv_ref[k]
        sw, sg = s_ref[0, k], s_ref[1, k]
        so = 1.0 - sw - sg
        m = mobilities(sw, sg)
        words = bits_ref[k]
        sat = (sw, so, sg)
        st = pv * (sw * COMPRESS[0] + so * COMPRESS[1] + sg * COMPRESS[2])
        storage[k] = st
        res = [pv * sat[a] * (1.0 + COMPRESS[a] * p) - om_ref[a, k] for a in range(3)]
        flux, coupling = face(
            p, m, jnp.where(lane2 < COLS - 1, tr_ref[2, k], 0.0), words,
            pltpu.roll(p, COLS - 1, 1), [pltpu.roll(x, COLS - 1, 1) for x in m], 6,
        )
        res = [res[a] + (flux[a] - pltpu.roll(flux[a], 1, 1)) for a in range(3)]
        back = pltpu.roll(coupling, 1, 1)
        cyu[k] = coupling
        cyd[k] = back
        inv[k] = st + (coupling + back)
        for a in range(3):
            res_ref[a, k] = res[a]
        if k > 0:
            flux, coupling = face(
                p_ref[k - 1], mobilities(s_ref[0, k - 1], s_ref[1, k - 1]), tr_ref[0, k - 1],
                bits_ref[k - 1], p, m, 0,
            )
            cz[k] = coupling
            inv[k] += coupling
            inv[k - 1] += coupling
            for a in range(3):
                res_ref[a, k] -= flux[a]
                res_ref[a, k - 1] += flux[a]

    pl.semaphore_wait(barrier, n_sector - 1 + n_slab - 1)

    halo_copies = [
        copy(dn_stage, halo_hi, h_ss.at[1], h_rs.at[1], (me, t_prev)),
        copy(rup_stage, rhalo_lo, h_ss.at[2], h_rs.at[2], (s_next, t)),
        copy(rdn_stage, rhalo_hi, h_ss.at[3], h_rs.at[3], (s_prev, t)),
    ]
    for c in halo_copies:
        c.start()
    for d in range(others):
        fault_copy(d).start()

    zero_tile = jnp.zeros((CHUNKS, 128), F32)
    layer_source = [zero_tile] * LAYERS
    take(far, f_rs.at[0])
    for d in range(others):
        flags = fup[d]
        w = fweight[d]
        flux, coupling = face(
            own[d, 0], mobilities(own[d, 1], own[d, 2]), w, flags,
            far[d, 0], mobilities(far[d, 1], far[d, 2]), 0,
        )
        for a in range(3):
            vals[d, a] = flux[a]
        vals[d, 3] = coupling
        link[d] = coupling
        layer = jnp.right_shift(cell[d], 13)
        total = flux[0] + flux[1] + flux[2]
        for k in range(LAYERS):
            layer_source[k] = layer_source[k] - jnp.where(layer == k, total, 0.0)

    nt = (((1,), (1,)), ((), ()))

    def masked(d, field):
        pieces = []
        for b in range(CHUNKS):
            mask = ohlo[d, :, b * 128 : (b + 1) * 128]
            parts = split(field[b : b + 1, :], 2)
            pieces.append(jnp.concatenate([mask * x for x in parts], 0))
        return jnp.concatenate(pieces, 1)

    def scatter(fields):
        total = None
        for d in range(others):
            rows = jnp.concatenate([masked(d, vals.at[d, i]) for i in fields], 0)
            part = lax.dot_general(rows, oh[d], nt, preferred_element_type=F32)
            total = part if total is None else total + part
        return [
            (total[256 * i : 256 * i + 128] + total[256 * i + 128 : 256 * i + 256])
            .T.reshape(LAYERS, ROWS, COLS)
            for i in range(len(fields))
        ]

    for c in halo_copies:
        c.wait_recv()

    p = p_ref[top]
    m = mobilities(s_ref[0, top], s_ref[1, top])
    flux, coupling = face(
        p, m, tr_ref[0, top] * not_last_slab, bits_ref[top],
        halo_hi[0], mobilities(halo_hi[1], halo_hi[2]), 0,
    )
    cz[LAYERS] = coupling
    inv[top] += coupling
    for a in range(3):
        res_ref[a, top] += flux[a]
        up_stage[a] = flux[a]
    up_stage[3] = coupling
    asend[12:13, :] = jnp.sum(flux[0] + flux[1] + flux[2], axis=0, keepdims=True)
    asend[13:16, :] = jnp.zeros((3, 128), F32)
    up_copy = copy(up_stage, halo_lo, h_ss.at[0], h_rs.at[0], (me, t_next))

    first_p = rdn_stage[0]
    low_flux, low_link = face(
        rhalo_lo[0], mobilities(rhalo_lo[1], rhalo_lo[2]), rhalo_lo[3] * not_first_sector,
        rhalo_lo[4].astype(jnp.int32), first_p, mobilities(rdn_stage[1], rdn_stage[2]), 3,
    )
    hi_m = mobilities(rhalo_hi[1], rhalo_hi[2])
    for k in range(LAYERS):
        p = p_ref[k]
        m = mobilities(s_ref[0, k], s_ref[1, k])

        def after(x, edge):
            return jnp.where(row2 == last, edge[k : k + 1], pltpu.roll(x, last, 0))

        def before(x, edge):
            return jnp.where(row2 == 0, edge[k : k + 1], pltpu.roll(x, 1, 0))

        weight = tr_ref[1, k] * jnp.where(row2 == last, not_last_sector, 1.0)
        flux, coupling = face(
            p, m, weight, bits_ref[k], after(p, rhalo_hi[0]),
            [after(m[a], hi_m[a]) for a in range(3)], 3,
        )
        back = before(coupling, low_link)
        cxu[k] = coupling
        cxd[k] = back
        inv[k] += coupling + back
        for a in range(3):
            res_ref[a, k] += flux[a] - before(flux[a], low_flux[a])

    for k in range(LAYERS):
        regular = -(res_ref[0, k] + res_ref[1, k] + res_ref[2, k])
        source = jnp.sum(regular, axis=0, keepdims=True) + jnp.sum(
            layer_source[k], axis=0, keepdims=True
        )
        asend[k : k + 1, :] = jnp.sum(storage[k], axis=0, keepdims=True)
        asend[4 + k : 5 + k, :] = jnp.sum(cz[k + 1], axis=0, keepdims=True)
        asend[8 + k : 9 + k, :] = source

    def a_copy(d):
        return copy(asend, arecv.at[mirror[d]], a_ss.at[0], a_rs.at[0],
                    (sector_of(d), t))

    for d in range(others):
        a_copy(d).start()
    up_copy.start()

    placed = scatter((0, 1))
    res_ref[0] += placed[0]
    res_ref[1] += placed[1]

    sums = asend[...]
    take(arecv, a_rs.at[0])
    for d in range(others):
        sums = sums + arecv[d]
    column = jnp.sum(sums, axis=1, keepdims=True)
    lane16 = lax.broadcasted_iota(jnp.int32, (16, 128), 1)
    row16 = lax.broadcasted_iota(jnp.int32, (16, 128), 0)
    spread = jnp.where(
        jnp.bitwise_and(lane16, 3) == jnp.bitwise_and(row16, 3),
        jnp.broadcast_to(column, (16, 128)), 0.0,
    )
    for q in range(4):
        bsend[q : q + 1, :] = jnp.sum(spread[4 * q : 4 * q + 4], axis=0, keepdims=True)
    brecv[t] = bsend[...]

    def b_copy(k, dst):
        return copy(bsend, brecv.at[dst], b_ss.at[0], b_rs.at[0],
                    (me, lax.rem(t + k, n_slab)))

    def hops(k):
        z, y, across = k % 8, k // 8, n_slab // 8
        return min(z, 8 - z) + min(y, across - y)

    for k in sorted(range(1, n_slab), key=lambda k: (-hops(k), k)):
        b_copy(k, t).start()

    placed = scatter((2, 3))
    res_ref[2] += placed[0]
    inv[...] += placed[1]
    up_copy.wait_recv()
    cz[0] = halo_lo[3]
    inv[0] += halo_lo[3]
    for a in range(3):
        res_ref[a, 0] -= halo_lo[a]
    inv[...] = RELAXATION / inv[...]
    for k in range(LAYERS):
        rhs[k] = -(res_ref[0, k] + res_ref[1, k] + res_ref[2, k])

    take(brecv.at[pl.ds(0, n_slab - 1)], b_rs.at[0])

    lane4 = lax.broadcasted_iota(jnp.int32, (4, 128), 1)
    rows = jnp.zeros((4, 128), F32)
    for j in range(n_slab):
        rows = rows + jnp.where(jnp.right_shift(lane4, 2) == j, brecv[j], 0.0)
    s_row, right = rows[0:1], rows[1:2]
    rhs_row = rows[2:3] + pltpu.roll(rows[3:4], LAYERS, 1)
    lane1 = lax.broadcasted_iota(jnp.int32, (1, 128), 1)
    right = jnp.where(lane1 < LAYERS * n_slab - 1, right, 0.0)
    s_row = jnp.where(lane1 < LAYERS * n_slab, s_row, 1.0)
    left = jnp.where(lane1 > 0, pltpu.roll(right, 1, 1), 0.0)
    step = 1
    while step < LAYERS * n_slab:
        pivot = 1.0 / (s_row + left + right)
        sn, ln, rn, dn = s_row * pivot, left * pivot, right * pivot, rhs_row * pivot
        s_row = s_row + left * pltpu.roll(sn, step, 1) + right * pltpu.roll(sn, 128 - step, 1)
        rhs_row = rhs_row + left * pltpu.roll(dn, step, 1) + right * pltpu.roll(dn, 128 - step, 1)
        left = left * pltpu.roll(ln, step, 1)
        right = right * pltpu.roll(rn, 128 - step, 1)
        step *= 2
    coarse = rhs_row / s_row
    lane8 = lax.broadcasted_iota(jnp.int32, (8, 128), 1)
    row8 = lax.broadcasted_iota(jnp.int32, (8, 128), 0)
    level = jnp.sum(
        jnp.where(lane8 == row8 + (LAYERS * t - 1), jnp.broadcast_to(coarse, (8, 128)), 0.0),
        axis=1, keepdims=True,
    )
    level = jnp.broadcast_to(level, (8, 128))

    def level_row(k):
        return level[k + 1 : k + 2]

    def place(partners_now, values, total):
        for d in partners_now:
            vals[d, 0] = link[d] * values(d)
            placed = lax.dot_general(
                oh[d], masked(d, vals.at[d, 0]), nt, preferred_element_type=F32
            )
            total = placed if total is None else total + placed
        return total

    def extra_of(total):
        return (total[:, :128] + total[:, 128:]).reshape(LAYERS, ROWS, COLS)

    def coarse_far(d):
        value = zero_tile
        for k in range(LAYERS):
            value = jnp.where(far[d, 3] == k, level_row(k), value)
        return value

    part[...] = extra_of(place(range(others), coarse_far, None))
    for k in range(LAYERS):
        here = level_row(k)
        total = part[k] + rhs[k] + cz[k + 1] * level_row(k + 1) + cz[k] * level_row(k - 1)
        total = total + (cxu[k] + cxd[k] + cyu[k] + cyd[k]) * here
        ubufs[0, k] = (1.0 - RELAXATION) * here + inv[k] * total

    groups = [list(range(2)), list(range(2, 4)), list(range(4, others))]
    group_of = {d: g for g, group in enumerate(groups) for d in group}
    for sweep in range(SWEEPS - 1):
        ubuf = ubufs.at[sweep]
        edge_copies = [
            copy(ubufs.at[sweep, top], zlo.at[sweep], w_ss.at[0], w_rs.at[sweep, 0], (me, t_next)),
            copy(ubufs.at[sweep, 0], zhi.at[sweep], w_ss.at[0], w_rs.at[sweep, 1], (me, t_prev)),
            copy(xup.at[sweep], xlo.at[sweep], w_ss.at[1], w_rs.at[sweep, 2], (s_next, t)),
            copy(xdn.at[sweep], xhi.at[sweep], w_ss.at[2], w_rs.at[sweep, 3], (s_prev, t)),
        ]
        edge_copies[0].start()
        edge_copies[1].start()
        flipped = ubuf[...].reshape(CELLS_HI, COLS).T
        weights = jnp.concatenate(split(flipped, 2), 0)
        fsplit[0, :256, :] = weights

        def u_copy(d, sweep=sweep):
            return copy(
                uown.at[sweep, d], urecv.at[sweep, mirror[d]],
                u_ss.at[0], u_rs.at[sweep, group_of[d]], (sector_of(d), t),
            )

        weights = fsplit[0, :256]
        for group in groups:
            for d in group:

                def store(i, b, row, d=d):
                    uown[sweep, d, b : b + 1, :] = row

                gather(d, [weights], 2, store)
            if group is groups[1]:
                for k in range(LAYERS):
                    xup[sweep, k : k + 1, :] = ubuf[k, last:]
                    xdn[sweep, k : k + 1, :] = ubuf[k, :1]
            for d in group:
                u_copy(d).start()
            if group is groups[1]:
                edge_copies[2].start()
                edge_copies[3].start()

        for k in range(LAYERS):
            u = ubuf[k]
            total = rhs[k] + cyu[k] * pltpu.roll(u, COLS - 1, 1) + cyd[k] * pltpu.roll(u, 1, 1)
            total = total + cxu[k] * jnp.where(row2 == last, 0.0, pltpu.roll(u, last, 0))
            total = total + cxd[k] * jnp.where(row2 == 0, 0.0, pltpu.roll(u, 1, 0))
            if k > 0:
                total = total + cz[k] * ubuf[k - 1]
            if k < top:
                total = total + cz[k + 1] * ubuf[k + 1]
            part[k] = total

        total = None
        for g, group in enumerate(groups):
            take(urecv.at[sweep, pl.ds(0, len(group))], u_rs.at[sweep, g])
            total = place([mirror[i] for i in group], lambda d: urecv[sweep, d], total)
        extra = extra_of(total)
        for c in edge_copies:
            c.wait_recv()
        part[0] += cz[0] * zlo[sweep]
        part[top] += cz[LAYERS] * zhi[sweep]
        for k in range(LAYERS):
            part[k, last:] += cxu[k, last:] * xhi[sweep, k : k + 1, :]
            part[k, :1] += cxd[k, :1] * xlo[sweep, k : k + 1, :]
        target = out_ref if sweep == SWEEPS - 2 else ubufs.at[sweep + 1]
        for k in range(LAYERS):
            target[k] = (1.0 - RELAXATION) * ubuf[k] + inv[k] * (part[k] + extra[k])

    for c in halo_copies + [up_copy]:
        c.wait_send()
    sent(far, f_ss.at[0])
    sent(arecv, a_ss.at[0])
    sent(brecv.at[pl.ds(0, n_slab - 1)], b_ss.at[0])
    sent(urecv, u_ss.at[0])
    sent(ubufs.at[:, pl.ds(0, 2)], w_ss.at[0])
    sent(xup, w_ss.at[1])
    sent(xdn, w_ss.at[2])


def body(n_sector, n_slab, *args):
    vmem = pl.BlockSpec(memory_space=pltpu.VMEM)
    others = n_sector - 1
    rounds = SWEEPS - 1
    block = (LAYERS, ROWS, COLS)
    tiles = (CHUNKS, 128)

    def f32(*shape):
        return pltpu.VMEM(shape, F32)

    def i32(*shape):
        return pltpu.VMEM(shape, jnp.int32)

    def sem(*shape):
        return pltpu.SemaphoreType.DMA(shape)

    scratch = dict(
        p_ref=f32(*block),
        s_ref=f32(2, *block),
        om_ref=f32(3, *block),
        pv_ref=f32(*block),
        tr_ref=f32(3, *block),
        bits_ref=i32(*block),
        fc_ref=i32(1, 1, n_sector, SLOTS),
        cnt_ref=pltpu.SMEM((1, 1, n_sector), jnp.int32),
        ft_ref=f32(1, 1, n_sector, SLOTS),
        fu_ref=i32(1, 1, n_sector, SLOTS),
        in_sem=sem(10),
        oh=pltpu.VMEM((others, CELLS_HI, SLOTS), BF),
        ohlo=pltpu.VMEM((others, 128, SLOTS), BF),
        fsplit=pltpu.VMEM((3, 384, CELLS_HI), BF),
        cell=i32(others, *tiles),
        fweight=f32(others, *tiles),
        fup=i32(others, *tiles),
        own=f32(others, 4, *tiles),
        far=f32(others, 4, *tiles),
        link=f32(others, *tiles),
        vals=f32(others, 4, *tiles),
        up_stage=f32(4, ROWS, COLS),
        dn_stage=f32(3, ROWS, COLS),
        halo_lo=f32(4, ROWS, COLS),
        halo_hi=f32(3, ROWS, COLS),
        rup_stage=f32(5, LAYERS, COLS),
        rdn_stage=f32(3, LAYERS, COLS),
        rhalo_lo=f32(5, LAYERS, COLS),
        rhalo_hi=f32(3, LAYERS, COLS),
        asend=f32(16, 128),
        arecv=f32(others, 16, 128),
        bsend=f32(4, 128),
        brecv=f32(n_slab, 4, 128),
        cz=f32(LAYERS + 1, ROWS, COLS),
        cxu=f32(*block),
        cxd=f32(*block),
        cyu=f32(*block),
        cyd=f32(*block),
        storage=f32(*block),
        rhs=f32(*block),
        inv=f32(*block),
        ubufs=f32(rounds, *block),
        part=f32(*block),
        uown=f32(rounds, others, *tiles),
        urecv=f32(rounds, others, *tiles),
        zlo=f32(rounds, ROWS, COLS),
        zhi=f32(rounds, ROWS, COLS),
        xup=f32(rounds, LAYERS, COLS),
        xdn=f32(rounds, LAYERS, COLS),
        xlo=f32(rounds, LAYERS, COLS),
        xhi=f32(rounds, LAYERS, COLS),
        f_ss=sem(1), f_rs=sem(1),
        h_ss=sem(4), h_rs=sem(4),
        a_ss=sem(1), a_rs=sem(1),
        b_ss=sem(1), b_rs=sem(1),
        u_ss=sem(1), u_rs=sem(rounds, 3),
        w_ss=sem(3), w_rs=sem(rounds, 4),
    )
    names = list(scratch)

    def run(*refs):
        kernel(n_sector, n_slab, refs[:10], *refs[10:12], **dict(zip(names, refs[12:])))

    return pl.pallas_call(
        run,
        out_shape=(
            jax.ShapeDtypeStruct((3, *block), F32),
            jax.ShapeDtypeStruct(block, F32),
        ),
        in_specs=[pl.BlockSpec(memory_space=pltpu.HBM)] * 10,
        out_specs=(vmem, vmem),
        scratch_shapes=list(scratch.values()),
        compiler_params=pltpu.CompilerParams(
            collective_id=0, has_side_effects=True, vmem_limit_bytes=60 * 2**20
        ),
    )(*args)


def solution(mesh):
    placed = (
        P("slab", "sector", None),
        P(None, "slab", "sector", None),
        P(None, "slab", "sector", None),
        P("slab", "sector", None),
        P(None, "slab", "sector", None),
        P("slab", "sector", None),
        P("slab", "sector", None, None),
        P("slab", "sector", None),
        P("slab", "sector", None, None),
        P("slab", "sector", None, None),
    )
    return jax.shard_map(
        functools.partial(body, mesh.shape["sector"], mesh.shape["slab"]),
        mesh=mesh,
        in_specs=placed,
        out_specs=(P(None, "slab", "sector", None), P("slab", "sector", None)),
        check_vma=False,
    )
```

```python
import functools

import jax
import jax.numpy as jnp
from jax import lax
from jax.experimental import pallas as pl
from jax.experimental.pallas import tpu as pltpu
from jax.sharding import PartitionSpec as P

COMPRESS = (0.0002, 0.0005, 0.002)
VISCOSITY = (1.0, 3.0, 0.5)
RELAXATION = 2.0 / 3.0
SWEEPS = 4

BF = jnp.bfloat16
F32 = jnp.float32
MESH = pl.DeviceIdType.MESH

LAYERS, ROWS, COLS = 4, 64, 128
CELLS_HI = LAYERS * ROWS
SLOTS = 1024
CHUNKS = SLOTS // 128


def split(value, count):
    parts = []
    for _ in range(count - 1):
        part = value.astype(BF)
        parts.append(part)
        value = value - part.astype(F32)
    parts.append(value.astype(BF))
    return parts


def mobilities(s_water, s_gas):
    s_oil = 1.0 - s_water - s_gas
    return [s * s * (1.0 / v) for s, v in zip((s_water, s_oil, s_gas), VISCOSITY)]


def face(p_low, m_low, weight, words, p_high, m_high, first_bit):
    drop = p_low - p_high
    fluxes, total = [], None
    for a in range(3):
        flag = jnp.bitwise_and(words, 1 << (first_bit + a)) != 0
        part = weight * jnp.where(flag, m_low[a], m_high[a])
        fluxes.append(part * drop)
        total = part if total is None else total + part
    return fluxes, total


def kernel(
    n_sector, n_slab,
    inputs, res_ref, out_ref, *,
    p_ref, s_ref, om_ref, pv_ref, tr_ref, bits_ref, fc_ref, cnt_ref, ft_ref, fu_ref, in_sem,
    oh, ohlo, fsplit, cell, fweight, fup, own, far, link, vals,
    up_stage, dn_stage, halo_lo, halo_hi, rup_stage, rdn_stage, rhalo_lo, rhalo_hi,
    asend, arecv, bsend, brecv,
    cz, cxu, cxd, cyu, cyd, storage, rhs, inv, ubufs, part,
    uown, urecv, zlo, zhi, xup, xdn, xlo, xhi,
    f_ss, f_rs, h_ss, h_rs, a_ss, a_rs, b_ss, b_rs, u_ss, u_rs, w_ss, w_rs,
):
    me = lax.axis_index("sector")
    t = lax.axis_index("slab")
    others = n_sector - 1
    s_next = lax.rem(me + 1, n_sector)
    s_prev = lax.rem(me + n_sector - 1, n_sector)
    t_next = lax.rem(t + 1, n_slab)
    t_prev = lax.rem(t + n_slab - 1, n_slab)

    def copy(src, dst, ss, rs, device):
        return pltpu.make_async_remote_copy(
            src_ref=src, dst_ref=dst, send_sem=ss, recv_sem=rs,
            device_id=device, device_id_type=MESH,
        )

    chips = n_sector // 2
    reach = sorted(range(1, chips), key=lambda c: (-min(c, chips - c), c))
    partners = [(c, other) for c in reach for other in (0, 1)] + [(0, 1)]
    mirror = [partners.index(((chips - c) % chips, other)) for c, other in partners]
    chip, core = me // 2, lax.rem(me, 2)

    sectors = [
        lax.rem(chip + c, chips) * 2 + (1 - core if other else core) for c, other in partners
    ]

    def sector_of(i):
        return sectors[i]

    def take(ref, sem):
        copy(ref, ref, sem, sem, (s_next, t)).wait_recv()

    def sent(ref, sem):
        copy(ref, ref, sem, sem, (s_next, t)).wait_send()

    held = (p_ref, s_ref, om_ref, pv_ref, tr_ref, bits_ref, fc_ref, cnt_ref, ft_ref, fu_ref)
    loads = [
        pltpu.make_async_copy(src, dst, in_sem.at[i])
        for i, (src, dst) in enumerate(zip(inputs, held))
    ]
    for i in (6, 7, 8, 9, 0, 1, 4, 5, 3, 2):
        loads[i].start()
    barrier = pltpu.get_barrier_semaphore()

    for i in range(others):
        pl.semaphore_signal(barrier, inc=1, device_id=(sector_of(i), t), device_id_type=MESH)

    @pl.loop(1, n_slab)
    def _(k):
        pl.semaphore_signal(
            barrier, inc=1, device_id=(me, lax.rem(t + k, n_slab)), device_id_type=MESH
        )

    for i in (6, 7, 8, 9, 0, 1, 4, 5):
        loads[i].wait()
    top = LAYERS - 1
    for i, plane in enumerate((p_ref[0], s_ref[0, 0], s_ref[1, 0])):
        dn_stage[i] = plane
    last = ROWS - 1
    for k in range(LAYERS):
        for i, row in enumerate(
            (p_ref[k, last:], s_ref[0, k, last:], s_ref[1, k, last:], tr_ref[1, k, last:])
        ):
            rup_stage[i, k : k + 1, :] = row
        rup_stage[4, k : k + 1, :] = bits_ref[k, last:].astype(F32)
        for i, row in enumerate((p_ref[k, :1], s_ref[0, k, :1], s_ref[1, k, :1])):
            rdn_stage[i, k : k + 1, :] = row

    lane = lax.broadcasted_iota(jnp.int32, (1, 128), 1)
    counts = [cnt_ref[0, 0, sector_of(d)] for d in range(others)]
    turn = lax.rem(n_sector - 2 * chip, n_sector)
    first_core = core == 0
    for b in range(CHUNKS):
        span = slice(b * 128, (b + 1) * 128)
        cells = pltpu.roll(fc_ref[0, 0, :, span], turn, 0)
        flags = pltpu.roll(fu_ref[0, 0, :, span], turn, 0)
        trans = pltpu.roll(ft_ref[0, 0, :, span], turn, 0)
        for d, (c, other) in enumerate(partners):
            here, there = 2 * c + other, 2 * c + 1 - other

            def pick(x):
                return jnp.where(first_core, x[here : here + 1], x[there : there + 1])

            cell[d, b : b + 1, :] = pick(cells)
            fup[d, b : b + 1, :] = pick(flags)
            fweight[d, b : b + 1, :] = jnp.where(lane + b * 128 < counts[d], pick(trans), 0.0)

    for i, field in enumerate((p_ref, s_ref.at[0], s_ref.at[1])):
        flipped = field[...].reshape(CELLS_HI, COLS).T
        for j, piece in enumerate(split(flipped, 3)):
            fsplit[i, j * 128 : (j + 1) * 128, :] = piece

    sub = lax.broadcasted_iota(jnp.int32, (128, 128), 0)
    sub_hi = lax.broadcasted_iota(jnp.int32, (CELLS_HI, 128), 0)

    @pl.loop(0, others)
    def _(d):
        for b in range(CHUNKS):
            span = slice(b * 128, (b + 1) * 128)
            c = cell[d, b : b + 1, :]
            oh[d, :, span] = jnp.where(sub_hi == jnp.right_shift(c, 7), 1.0, 0.0).astype(BF)
            ohlo[d, :, span] = jnp.where(sub == jnp.bitwise_and(c, 127), 1.0, 0.0).astype(BF)

    def gather(d, weights, count, store):
        rows = [jnp.bitwise_and(cell[d, b : b + 1, :], 127) for b in range(CHUNKS)]
        for i, w in enumerate(weights):
            for b in range(CHUNKS // 2):
                picks = oh[d, :, b * 256 : (b + 1) * 256]
                g = jnp.dot(w, picks, preferred_element_type=F32)
                total = g[(count - 1) * 128 :]
                for j in reversed(range(count - 1)):
                    total = g[j * 128 : (j + 1) * 128] + total
                for k in range(2):
                    found = jnp.where(
                        sub == rows[2 * b + k], total[:, k * 128 : (k + 1) * 128], 0.0
                    )
                    store(i, 2 * b + k, jnp.sum(found, axis=0, keepdims=True))

    def fault_copy(d):
        return copy(own.at[d], far.at[mirror[d]], f_ss.at[0], f_rs.at[0],
                    (sector_of(d), t))

    for d in range(others):

        def store(i, b, row, d=d):
            own[d, i, b : b + 1, :] = row

        gather(d, [fsplit[i] for i in range(3)], 3, store)
        own[d, 3] = jnp.right_shift(cell[d], 13).astype(F32)

    lane2 = lax.broadcasted_iota(jnp.int32, (ROWS, COLS), 1)
    row2 = lax.broadcasted_iota(jnp.int32, (ROWS, COLS), 0)
    not_first_slab = jnp.where(t > 0, 1.0, 0.0).astype(F32)
    not_last_slab = jnp.where(t < n_slab - 1, 1.0, 0.0).astype(F32)
    not_first_sector = jnp.where(me > 0, 1.0, 0.0).astype(F32)
    not_last_sector = jnp.where(me < n_sector - 1, 1.0, 0.0).astype(F32)

    loads[3].wait()
    loads[2].wait()
    for k in range(LAYERS):
        p = p_ref[k]
        pv = pv_ref[k]
        sw, sg = s_ref[0, k], s_ref[1, k]
        so = 1.0 - sw - sg
        m = mobilities(sw, sg)
        words = bits_ref[k]
        sat = (sw, so, sg)
        st = pv * (sw * COMPRESS[0] + so * COMPRESS[1] + sg * COMPRESS[2])
        storage[k] = st
        res = [pv * sat[a] * (1.0 + COMPRESS[a] * p) - om_ref[a, k] for a in range(3)]
        flux, coupling = face(
            p, m, jnp.where(lane2 < COLS - 1, tr_ref[2, k], 0.0), words,
            pltpu.roll(p, COLS - 1, 1), [pltpu.roll(x, COLS - 1, 1) for x in m], 6,
        )
        res = [res[a] + (flux[a] - pltpu.roll(flux[a], 1, 1)) for a in range(3)]
        back = pltpu.roll(coupling, 1, 1)
        cyu[k] = coupling
        cyd[k] = back
        inv[k] = st + (coupling + back)
        for a in range(3):
            res_ref[a, k] = res[a]
        if k > 0:
            flux, coupling = face(
                p_ref[k - 1], mobilities(s_ref[0, k - 1], s_ref[1, k - 1]), tr_ref[0, k - 1],
                bits_ref[k - 1], p, m, 0,
            )
            cz[k] = coupling
            inv[k] += coupling
            inv[k - 1] += coupling
            for a in range(3):
                res_ref[a, k] -= flux[a]
                res_ref[a, k - 1] += flux[a]

    pl.semaphore_wait(barrier, n_sector - 1 + n_slab - 1)

    halo_copies = [
        copy(dn_stage, halo_hi, h_ss.at[1], h_rs.at[1], (me, t_prev)),
        copy(rup_stage, rhalo_lo, h_ss.at[2], h_rs.at[2], (s_next, t)),
        copy(rdn_stage, rhalo_hi, h_ss.at[3], h_rs.at[3], (s_prev, t)),
    ]
    for c in halo_copies:
        c.start()
    for d in range(others):
        fault_copy(d).start()

    zero_tile = jnp.zeros((CHUNKS, 128), F32)
    layer_source = [zero_tile] * LAYERS
    take(far, f_rs.at[0])
    for d in range(others):
        flags = fup[d]
        w = fweight[d]
        flux, coupling = face(
            own[d, 0], mobilities(own[d, 1], own[d, 2]), w, flags,
            far[d, 0], mobilities(far[d, 1], far[d, 2]), 0,
        )
        for a in range(3):
            vals[d, a] = flux[a]
        vals[d, 3] = coupling
        link[d] = coupling
        layer = jnp.right_shift(cell[d], 13)
        total = flux[0] + flux[1] + flux[2]
        for k in range(LAYERS):
            layer_source[k] = layer_source[k] - jnp.where(layer == k, total, 0.0)

    nt = (((1,), (1,)), ((), ()))

    def masked(d, field):
        pieces = []
        for b in range(CHUNKS):
            mask = ohlo[d, :, b * 128 : (b + 1) * 128]
            parts = split(field[b : b + 1, :], 2)
            pieces.append(jnp.concatenate([mask * x for x in parts], 0))
        return jnp.concatenate(pieces, 1)

    def scatter(fields):
        total = None
        for d in range(others):
            rows = jnp.concatenate([masked(d, vals.at[d, i]) for i in fields], 0)
            part = lax.dot_general(rows, oh[d], nt, preferred_element_type=F32)
            total = part if total is None else total + part
        return [
            (total[256 * i : 256 * i + 128] + total[256 * i + 128 : 256 * i + 256])
            .T.reshape(LAYERS, ROWS, COLS)
            for i in range(len(fields))
        ]

    for c in halo_copies:
        c.wait_recv()

    p = p_ref[top]
    m = mobilities(s_ref[0, top], s_ref[1, top])
    flux, coupling = face(
        p, m, tr_ref[0, top] * not_last_slab, bits_ref[top],
        halo_hi[0], mobilities(halo_hi[1], halo_hi[2]), 0,
    )
    cz[LAYERS] = coupling
    inv[top] += coupling
    for a in range(3):
        res_ref[a, top] += flux[a]
        up_stage[a] = flux[a]
    up_stage[3] = coupling
    asend[12:13, :] = jnp.sum(flux[0] + flux[1] + flux[2], axis=0, keepdims=True)
    asend[13:16, :] = jnp.zeros((3, 128), F32)
    up_copy = copy(up_stage, halo_lo, h_ss.at[0], h_rs.at[0], (me, t_next))

    first_p = rdn_stage[0]
    low_flux, low_link = face(
        rhalo_lo[0], mobilities(rhalo_lo[1], rhalo_lo[2]), rhalo_lo[3] * not_first_sector,
        rhalo_lo[4].astype(jnp.int32), first_p, mobilities(rdn_stage[1], rdn_stage[2]), 3,
    )
    hi_m = mobilities(rhalo_hi[1], rhalo_hi[2])
    for k in range(LAYERS):
        p = p_ref[k]
        m = mobilities(s_ref[0, k], s_ref[1, k])

        def after(x, edge):
            return jnp.where(row2 == last, edge[k : k + 1], pltpu.roll(x, last, 0))

        def before(x, edge):
            return jnp.where(row2 == 0, edge[k : k + 1], pltpu.roll(x, 1, 0))

        weight = tr_ref[1, k] * jnp.where(row2 == last, not_last_sector, 1.0)
        flux, coupling = face(
            p, m, weight, bits_ref[k], after(p, rhalo_hi[0]),
            [after(m[a], hi_m[a]) for a in range(3)], 3,
        )
        back = before(coupling, low_link)
        cxu[k] = coupling
        cxd[k] = back
        inv[k] += coupling + back
        for a in range(3):
            res_ref[a, k] += flux[a] - before(flux[a], low_flux[a])

    for k in range(LAYERS):
        regular = -(res_ref[0, k] + res_ref[1, k] + res_ref[2, k])
        source = jnp.sum(regular, axis=0, keepdims=True) + jnp.sum(
            layer_source[k], axis=0, keepdims=True
        )
        asend[k : k + 1, :] = jnp.sum(storage[k], axis=0, keepdims=True)
        asend[4 + k : 5 + k, :] = jnp.sum(cz[k + 1], axis=0, keepdims=True)
        asend[8 + k : 9 + k, :] = source

    def a_copy(d):
        return copy(asend, arecv.at[mirror[d]], a_ss.at[0], a_rs.at[0],
                    (sector_of(d), t))

    for d in range(others):
        a_copy(d).start()
    up_copy.start()

    placed = scatter((0, 1))
    res_ref[0] += placed[0]
    res_ref[1] += placed[1]

    sums = asend[...]
    take(arecv, a_rs.at[0])
    for d in range(others):
        sums = sums + arecv[d]
    column = jnp.sum(sums, axis=1, keepdims=True)
    lane16 = lax.broadcasted_iota(jnp.int32, (16, 128), 1)
    row16 = lax.broadcasted_iota(jnp.int32, (16, 128), 0)
    spread = jnp.where(
        jnp.bitwise_and(lane16, 3) == jnp.bitwise_and(row16, 3),
        jnp.broadcast_to(column, (16, 128)), 0.0,
    )
    for q in range(4):
        bsend[q : q + 1, :] = jnp.sum(spread[4 * q : 4 * q + 4], axis=0, keepdims=True)
    brecv[t] = bsend[...]

    def b_copy(k, dst):
        return copy(bsend, brecv.at[dst], b_ss.at[0], b_rs.at[0],
                    (me, lax.rem(t + k, n_slab)))

    def hops(k):
        z, y, across = k % 8, k // 8, n_slab // 8
        return min(z, 8 - z) + min(y, across - y)

    for k in sorted(range(1, n_slab), key=lambda k: (-hops(k), k)):
        b_copy(k, t).start()

    placed = scatter((2, 3))
    res_ref[2] += placed[0]
    inv[...] += placed[1]
    up_copy.wait_recv()
    cz[0] = halo_lo[3]
    inv[0] += halo_lo[3]
    for a in range(3):
        res_ref[a, 0] -= halo_lo[a]
    inv[...] = RELAXATION / inv[...]
    for k in range(LAYERS):
        rhs[k] = -(res_ref[0, k] + res_ref[1, k] + res_ref[2, k])

    take(brecv.at[pl.ds(0, n_slab - 1)], b_rs.at[0])

    lane4 = lax.broadcasted_iota(jnp.int32, (4, 128), 1)
    rows = jnp.zeros((4, 128), F32)
    for j in range(n_slab):
        rows = rows + jnp.where(jnp.right_shift(lane4, 2) == j, brecv[j], 0.0)
    s_row, right = rows[0:1], rows[1:2]
    rhs_row = rows[2:3] + pltpu.roll(rows[3:4], LAYERS, 1)
    lane1 = lax.broadcasted_iota(jnp.int32, (1, 128), 1)
    right = jnp.where(lane1 < LAYERS * n_slab - 1, right, 0.0)
    s_row = jnp.where(lane1 < LAYERS * n_slab, s_row, 1.0)
    left = jnp.where(lane1 > 0, pltpu.roll(right, 1, 1), 0.0)
    step = 1
    while step < LAYERS * n_slab:
        pivot = 1.0 / (s_row + left + right)
        sn, ln, rn, dn = s_row * pivot, left * pivot, right * pivot, rhs_row * pivot
        s_row = s_row + left * pltpu.roll(sn, step, 1) + right * pltpu.roll(sn, 128 - step, 1)
        rhs_row = rhs_row + left * pltpu.roll(dn, step, 1) + right * pltpu.roll(dn, 128 - step, 1)
        left = left * pltpu.roll(ln, step, 1)
        right = right * pltpu.roll(rn, 128 - step, 1)
        step *= 2
    coarse = rhs_row / s_row
    lane8 = lax.broadcasted_iota(jnp.int32, (8, 128), 1)
    row8 = lax.broadcasted_iota(jnp.int32, (8, 128), 0)
    level = jnp.sum(
        jnp.where(lane8 == row8 + (LAYERS * t - 1), jnp.broadcast_to(coarse, (8, 128)), 0.0),
        axis=1, keepdims=True,
    )
    level = jnp.broadcast_to(level, (8, 128))

    def level_row(k):
        return level[k + 1 : k + 2]

    def place(partners_now, values, total):
        for d in partners_now:
            vals[d, 0] = link[d] * values(d)
            placed = lax.dot_general(
                oh[d], masked(d, vals.at[d, 0]), nt, preferred_element_type=F32
            )
            total = placed if total is None else total + placed
        return total

    def extra_of(total):
        return (total[:, :128] + total[:, 128:]).reshape(LAYERS, ROWS, COLS)

    def coarse_far(d):
        value = zero_tile
        for k in range(LAYERS):
            value = jnp.where(far[d, 3] == k, level_row(k), value)
        return value

    part[...] = extra_of(place(range(others), coarse_far, None))
    for k in range(LAYERS):
        here = level_row(k)
        total = part[k] + rhs[k] + cz[k + 1] * level_row(k + 1) + cz[k] * level_row(k - 1)
        total = total + (cxu[k] + cxd[k] + cyu[k] + cyd[k]) * here
        ubufs[0, k] = (1.0 - RELAXATION) * here + inv[k] * total

    groups = [list(range(2)), list(range(2, 4)), list(range(4, others))]
    group_of = {d: g for g, group in enumerate(groups) for d in group}
    for sweep in range(SWEEPS - 1):
        ubuf = ubufs.at[sweep]
        edge_copies = [
            copy(ubufs.at[sweep, top], zlo.at[sweep], w_ss.at[0], w_rs.at[sweep, 0], (me, t_next)),
            copy(ubufs.at[sweep, 0], zhi.at[sweep], w_ss.at[0], w_rs.at[sweep, 1], (me, t_prev)),
            copy(xup.at[sweep], xlo.at[sweep], w_ss.at[1], w_rs.at[sweep, 2], (s_next, t)),
            copy(xdn.at[sweep], xhi.at[sweep], w_ss.at[2], w_rs.at[sweep, 3], (s_prev, t)),
        ]
        flipped = ubuf[...].reshape(CELLS_HI, COLS).T
        weights = jnp.concatenate(split(flipped, 2), 0)
        fsplit[0, :256, :] = weights

        def u_copy(d, sweep=sweep):
            return copy(
                uown.at[sweep, d], urecv.at[sweep, mirror[d]],
                u_ss.at[0], u_rs.at[sweep, group_of[d]], (sector_of(d), t),
            )

        weights = fsplit[0, :256]
        for group in groups:
            for d in group:

                def store(i, b, row, d=d):
                    uown[sweep, d, b : b + 1, :] = row

                gather(d, [weights], 2, store)
            if group is groups[1]:
                for k in range(LAYERS):
                    xup[sweep, k : k + 1, :] = ubuf[k, last:]
                    xdn[sweep, k : k + 1, :] = ubuf[k, :1]
            for d in group:
                u_copy(d).start()
            if group is groups[0]:
                edge_copies[0].start()
                edge_copies[1].start()
            if group is groups[1]:
                edge_copies[2].start()
                edge_copies[3].start()

        for k in range(LAYERS):
            u = ubuf[k]
            total = rhs[k] + cyu[k] * pltpu.roll(u, COLS - 1, 1) + cyd[k] * pltpu.roll(u, 1, 1)
            total = total + cxu[k] * jnp.where(row2 == last, 0.0, pltpu.roll(u, last, 0))
            total = total + cxd[k] * jnp.where(row2 == 0, 0.0, pltpu.roll(u, 1, 0))
            if k > 0:
                total = total + cz[k] * ubuf[k - 1]
            if k < top:
                total = total + cz[k + 1] * ubuf[k + 1]
            part[k] = total

        total = None
        for g, group in enumerate(groups):
            take(urecv.at[sweep, pl.ds(0, len(group))], u_rs.at[sweep, g])
            total = place([mirror[i] for i in group], lambda d: urecv[sweep, d], total)
        extra = extra_of(total)
        for c in edge_copies:
            c.wait_recv()
        part[0] += cz[0] * zlo[sweep]
        part[top] += cz[LAYERS] * zhi[sweep]
        for k in range(LAYERS):
            part[k, last:] += cxu[k, last:] * xhi[sweep, k : k + 1, :]
            part[k, :1] += cxd[k, :1] * xlo[sweep, k : k + 1, :]
        target = out_ref if sweep == SWEEPS - 2 else ubufs.at[sweep + 1]
        for k in range(LAYERS):
            target[k] = (1.0 - RELAXATION) * ubuf[k] + inv[k] * (part[k] + extra[k])

    for c in halo_copies + [up_copy]:
        c.wait_send()
    sent(far, f_ss.at[0])
    sent(arecv, a_ss.at[0])
    sent(brecv.at[pl.ds(0, n_slab - 1)], b_ss.at[0])
    sent(urecv, u_ss.at[0])
    sent(ubufs.at[:, pl.ds(0, 2)], w_ss.at[0])
    sent(xup, w_ss.at[1])
    sent(xdn, w_ss.at[2])


def body(n_sector, n_slab, *args):
    vmem = pl.BlockSpec(memory_space=pltpu.VMEM)
    others = n_sector - 1
    rounds = SWEEPS - 1
    block = (LAYERS, ROWS, COLS)
    tiles = (CHUNKS, 128)

    def f32(*shape):
        return pltpu.VMEM(shape, F32)

    def i32(*shape):
        return pltpu.VMEM(shape, jnp.int32)

    def sem(*shape):
        return pltpu.SemaphoreType.DMA(shape)

    scratch = dict(
        p_ref=f32(*block),
        s_ref=f32(2, *block),
        om_ref=f32(3, *block),
        pv_ref=f32(*block),
        tr_ref=f32(3, *block),
        bits_ref=i32(*block),
        fc_ref=i32(1, 1, n_sector, SLOTS),
        cnt_ref=pltpu.SMEM((1, 1, n_sector), jnp.int32),
        ft_ref=f32(1, 1, n_sector, SLOTS),
        fu_ref=i32(1, 1, n_sector, SLOTS),
        in_sem=sem(10),
        oh=pltpu.VMEM((others, CELLS_HI, SLOTS), BF),
        ohlo=pltpu.VMEM((others, 128, SLOTS), BF),
        fsplit=pltpu.VMEM((3, 384, CELLS_HI), BF),
        cell=i32(others, *tiles),
        fweight=f32(others, *tiles),
        fup=i32(others, *tiles),
        own=f32(others, 4, *tiles),
        far=f32(others, 4, *tiles),
        link=f32(others, *tiles),
        vals=f32(others, 4, *tiles),
        up_stage=f32(4, ROWS, COLS),
        dn_stage=f32(3, ROWS, COLS),
        halo_lo=f32(4, ROWS, COLS),
        halo_hi=f32(3, ROWS, COLS),
        rup_stage=f32(5, LAYERS, COLS),
        rdn_stage=f32(3, LAYERS, COLS),
        rhalo_lo=f32(5, LAYERS, COLS),
        rhalo_hi=f32(3, LAYERS, COLS),
        asend=f32(16, 128),
        arecv=f32(others, 16, 128),
        bsend=f32(4, 128),
        brecv=f32(n_slab, 4, 128),
        cz=f32(LAYERS + 1, ROWS, COLS),
        cxu=f32(*block),
        cxd=f32(*block),
        cyu=f32(*block),
        cyd=f32(*block),
        storage=f32(*block),
        rhs=f32(*block),
        inv=f32(*block),
        ubufs=f32(rounds, *block),
        part=f32(*block),
        uown=f32(rounds, others, *tiles),
        urecv=f32(rounds, others, *tiles),
        zlo=f32(rounds, ROWS, COLS),
        zhi=f32(rounds, ROWS, COLS),
        xup=f32(rounds, LAYERS, COLS),
        xdn=f32(rounds, LAYERS, COLS),
        xlo=f32(rounds, LAYERS, COLS),
        xhi=f32(rounds, LAYERS, COLS),
        f_ss=sem(1), f_rs=sem(1),
        h_ss=sem(4), h_rs=sem(4),
        a_ss=sem(1), a_rs=sem(1),
        b_ss=sem(1), b_rs=sem(1),
        u_ss=sem(1), u_rs=sem(rounds, 3),
        w_ss=sem(3), w_rs=sem(rounds, 4),
    )
    names = list(scratch)

    def run(*refs):
        kernel(n_sector, n_slab, refs[:10], *refs[10:12], **dict(zip(names, refs[12:])))

    return pl.pallas_call(
        run,
        out_shape=(
            jax.ShapeDtypeStruct((3, *block), F32),
            jax.ShapeDtypeStruct(block, F32),
        ),
        in_specs=[pl.BlockSpec(memory_space=pltpu.HBM)] * 10,
        out_specs=(vmem, vmem),
        scratch_shapes=list(scratch.values()),
        compiler_params=pltpu.CompilerParams(
            collective_id=0, has_side_effects=True, vmem_limit_bytes=60 * 2**20
        ),
    )(*args)


def solution(mesh):
    placed = (
        P("slab", "sector", None),
        P(None, "slab", "sector", None),
        P(None, "slab", "sector", None),
        P("slab", "sector", None),
        P(None, "slab", "sector", None),
        P("slab", "sector", None),
        P("slab", "sector", None, None),
        P("slab", "sector", None),
        P("slab", "sector", None, None),
        P("slab", "sector", None, None),
    )
    return jax.shard_map(
        functools.partial(body, mesh.shape["sector"], mesh.shape["slab"]),
        mesh=mesh,
        in_specs=placed,
        out_specs=(P(None, "slab", "sector", None), P("slab", "sector", None)),
        check_vma=False,
    )
```
